256 devices in a mesh: ra: 32 (over x, z_hi, y), dec: 8 (over z_lo, core).
Axes of the slice: x: 4, y: 4, z: 8 (z_hi: 2, z_lo: 4; z = z_hi * 4 + z_lo), core: 2. Of those that a mesh axis runs over, the one named last changes fastest.
Arguments:
- cube: float32 [32, 512, 4096], P('ra', 'dec'), may hold values from -40 to 40, as said below
Outputs:
- snr: float32 [3, 2, 32, 512, 4096], P(None, None, None, 'dec', 'ra')
The draws below stay inside these ranges and needn't reach their ends.
Inputs may be any that keep to these rules, and one draw needn't show every extreme that they name: A float cube.
All inputs are finite; a program needn't handle non-finite values.
Results may differ from the reference program's by a relative error of at most 0.00025.
Values sent between devices are 32-bit elements; how exact they have to be, the bound alone decides.
No kernel may reach another device: no remote copies, remote signals or barrier semaphores. Data moves between devices by JAX's collectives and lax.ppermute only.
A program may use at most 64 MiB of HBM per device.

```python
import jax
import jax.numpy as jnp
from jax import lax

CH = 32
NDEC = 512
NRA = 4096


def draw_cube(key, part):
    key = jax.random.fold_in(key, 11)
    key_noise = jax.random.fold_in(key, 1)
    key_chan = jax.random.fold_in(key, 2)
    key_pix = jax.random.fold_in(key, 3)
    channel_scale = jnp.exp(jax.random.uniform(key_chan, (CH, 1, 1), jnp.float32, 0.0, 2.302585))
    pixel_scale = jnp.exp(jax.random.uniform(key_pix, (1, NDEC, NRA), jnp.float32, 0.0, 2.302585))
    noise = jax.random.truncated_normal(key_noise, -4.0, 4.0, (CH, NDEC, NRA), jnp.float32)
    value = noise * channel_scale * pixel_scale / 10.0
    return value.astype(jnp.float32)


def setup_inputs(seed: int = 0) -> dict:
    keys = jax.random.split(jax.random.key(seed), 2)
    cube = draw_cube(jax.random.fold_in(keys[1], 71), 0)
    return {"cube": cube}


sigma_values = (1, 2, 4)
boxcar_widths = (3, 7)
epsilon = 1e-06

def smooth_along(field, sigma, axis):
    reach = 3 * sigma
    lags = jnp.arange(-reach, reach + 1).astype(jnp.float32)
    weights = jnp.exp(-lags * lags / (2.0 * sigma * sigma))
    weights = weights / jnp.sum(weights)
    length = field.shape[axis]
    widths = [(0, 0), (0, 0), (0, 0)]
    widths[axis] = (reach, reach)
    padded = jnp.pad(field, widths)
    total = jnp.zeros(field.shape, jnp.float32)
    for step in range(2 * reach + 1):
        total = total + weights[step] * lax.slice_in_dim(padded, step, step + length, axis=axis)
    return total

def reference(cube):
    results = []
    for sigma in sigma_values:
        smooth = smooth_along(smooth_along(cube, sigma, 2), sigma, 1)
        kernel_out = []
        for width in boxcar_widths:
            half = width // 2
            padded = jnp.pad(smooth, ((half, half), (0, 0), (0, 0)))
            summed = jnp.zeros(smooth.shape, jnp.float32)
            for step in range(width):
                summed = summed + padded[step:step + CH]
            summed = summed / width
            square = lax.optimization_barrier(jnp.sum(summed * summed, axis=0))
            framed = jnp.pad(square, 1)
            boxed = jnp.zeros(square.shape, jnp.float32)
            for row in range(3):
                for col in range(3):
                    boxed = boxed + framed[row:row + square.shape[0], col:col + square.shape[1]]
            noise = jnp.sqrt(boxed / (9.0 * CH) + epsilon)
            kernel_out.append(summed / noise)
        results.append(jnp.stack(kernel_out))
    return jnp.stack(results)
```

```python
import functools

import jax
import jax.numpy as jnp
import ml_dtypes
import numpy as np
from jax import lax
from jax.experimental import pallas as pl
from jax.experimental.pallas import tpu as pltpu
from jax.sharding import PartitionSpec as P

sigma_values = (1, 2, 4)
boxcar_widths = (3, 7)
epsilon = 1e-06

LANES = 128
ROWS = 64
EDGE = 16
SPAN = ROWS + 2 * EDGE
OUT = ROWS + 8
HALF = 40
CHUNK = 2 * HALF
edge_rows = tuple(range(0, EDGE)) + tuple(range(ROWS - EDGE, ROWS))
middle_rows = tuple(range(EDGE, ROWS - EDGE))
row_at = np.array(
    edge_rows + middle_rows + tuple(range(-EDGE, 0)) + tuple(range(ROWS, ROWS + EDGE))
)
col_at = np.array(tuple(range(LANES)) + tuple(range(LANES, LANES + 16)) + tuple(range(-16, 0)))


def taps(distance, sigma):
    reach = 3 * sigma
    lags = np.arange(-reach, reach + 1, dtype=np.float64)
    weight_sum = np.sum(np.exp(-lags * lags / (2.0 * sigma * sigma)))
    value = np.exp(-(distance.astype(np.float64) ** 2) / (2.0 * sigma * sigma)) / weight_sum
    return np.where(np.abs(distance) <= reach, value, 0.0).astype(np.float32)


def halves(value):
    high = value.astype(ml_dtypes.bfloat16)
    low = (value - high.astype(np.float32)).astype(ml_dtypes.bfloat16)
    return high, low


def ra_weights():
    weights = np.zeros((2 * LANES, 4 * LANES), np.float32)
    for s, sigma in enumerate(sigma_values):
        weights[: len(col_at), s * LANES : (s + 1) * LANES] = taps(
            col_at[:, None] - np.arange(LANES)[None, :], sigma
        )
        for side, col in enumerate((-1, LANES)):
            weights[: len(col_at), 3 * LANES + 32 * s + side] = taps(col_at - col, sigma)
    high, low = halves(weights)
    return np.concatenate([high, high], axis=0), low


def dec_weights():
    result = np.zeros((3, 2 * OUT, 2 * SPAN), ml_dtypes.bfloat16)
    out_at = np.concatenate([np.arange(ROWS), [-1, ROWS]])
    for s, sigma in enumerate(sigma_values):
        weights = np.zeros((OUT, SPAN), np.float32)
        weights[: ROWS + 2] = taps(row_at[None, :] - out_at[:, None], sigma)
        high, low = halves(weights)
        result[s, :OUT, :SPAN] = high
        result[s, :OUT, SPAN:] = high
        result[s, OUT:, :SPAN] = low
    return result


def edge_weights(channels):
    half = channels // 2
    lane = np.arange(2 * LANES)
    tile, within = lane // LANES, lane % LANES
    sigma, slot = within // 32, within % 32
    channel, side = tile * half + slot // 2, slot % 2
    used = (sigma < 3) & (slot < 2 * half)
    same = used[:, None] & used[None, :] & (sigma[:, None] == sigma[None, :])
    same &= side[:, None] == side[None, :]
    boxcars = [
        same & (np.abs(channel[:, None] - channel[None, :]) <= width // 2)
        for width in boxcar_widths
    ]
    gathers = np.zeros((3, 2 * LANES, LANES), bool)
    for s in range(3):
        gathers[s, :, 0] = used & (sigma == s) & (side == 0)
        gathers[s, :, LANES - 1] = used & (sigma == s) & (side == 1)
    return (
        np.stack(boxcars).astype(ml_dtypes.bfloat16),
        gathers.astype(ml_dtypes.bfloat16),
    )


def lane_index(shape):
    return lax.broadcasted_iota(jnp.int32, shape, len(shape) - 1)


def split(value):
    high = value.astype(jnp.bfloat16)
    low = (value - high.astype(jnp.float32)).astype(jnp.bfloat16)
    return high, low


def dot(a, b):
    return jnp.dot(a, b, preferred_element_type=jnp.float32)


def pack_kernel(cube_ref, out_ref):
    tiles = out_ref.shape[0]
    lane = lane_index((8, LANES))

    def block(tile, row):
        if tile < 0 or tile >= tiles:
            return jnp.zeros((8, LANES), jnp.float32)
        return cube_ref[0, row : row + 8, tile * LANES : (tile + 1) * LANES]

    for tile in range(tiles):
        for half, rows in enumerate((edge_rows, middle_rows)):
            packed = jnp.zeros((8, LANES), jnp.float32)
            for group in range(4):
                row = rows[8 * group]
                at = half * HALF + 8 * group
                out_ref[tile, at : at + 8, :] = block(tile, row)
                halo = jnp.where(
                    lane < 16,
                    block(tile + 1, row),
                    jnp.where(lane < 32, pltpu.roll(block(tile - 1, row), 32, 1), 0.0),
                )
                packed = packed + (pltpu.roll(halo, 32 * group, 1) if group else halo)
            out_ref[tile, half * HALF + 32 : (half + 1) * HALF, :] = packed


def edge_kernel(tile_ref, top_ref, bottom_ref):
    channels = tile_ref.shape[0]
    lane = lane_index((8, LANES))
    for c in range(channels):
        top_ref[c * EDGE : (c + 1) * EDGE, :] = tile_ref[c, :EDGE, :]
        bottom_ref[c * EDGE : (c + 1) * EDGE, :] = tile_ref[c, EDGE : 2 * EDGE, :]
    for pair in range(channels // 2):
        at = channels * EDGE + 8 * pair
        first = tile_ref[2 * pair, 32:HALF, :]
        second = tile_ref[2 * pair + 1, 32:HALF, :]
        top_ref[at : at + 8, :] = jnp.where(lane < 64, first, pltpu.roll(second, 64, 1))
        bottom_ref[at : at + 8, :] = jnp.where(lane < 64, pltpu.roll(first, 64, 1), second)


def snr_kernel(
    tile_ref, above_ref, below_ref, ra_both_ref, ra_low_ref, dec_ref, box_ref, gather_ref,
    out_ref,
    source, ra_done, smooth, result, edges, framed, sems,
    *, batch,
):
    channels = tile_ref.shape[0]
    ra_at, ra_n = lax.axis_index("ra"), lax.axis_size("ra")
    dec_at, dec_n = lax.axis_index("dec"), lax.axis_size("dec")
    half_c = channels // 2
    edges[...] = jnp.zeros_like(edges)

    def aligned(packed, lanes):
        return pltpu.roll(packed, LANES - lanes, 1) if lanes else packed

    def put(row, main, packed):
        for k, value in enumerate((main, packed)):
            high, low = split(value)
            source[pl.ds(row, 16), k * LANES : (k + 1) * LANES] = high
            source[pl.ds(row, 16), (2 + k) * LANES : (3 + k) * LANES] = low

    def smooth_ra(step, carry):
        for j in range(batch):
            c = step * batch + j
            base = j * SPAN
            for half in range(2):
                packed = tile_ref[c, half * HALF + 32 : (half + 1) * HALF, :]
                for k in range(2):
                    main = tile_ref[c, half * HALF + 16 * k : half * HALF + 16 * k + 16, :]
                    halo = jnp.concatenate(
                        [aligned(packed, 64 * k), aligned(packed, 64 * k + 32)], axis=0
                    )
                    put(base + 32 * half + 16 * k, main, halo)
            for k, ref in enumerate((above_ref, below_ref)):
                main = ref[pl.ds(pl.multiple_of(c * EDGE, EDGE), EDGE), :]
                pair = step * (batch // 2) + j // 2
                packed = ref[pl.ds(pl.multiple_of(channels * EDGE + 8 * pair, 8), 8), :]
                lanes = 64 * (j % 2)
                halo = jnp.concatenate([aligned(packed, lanes), aligned(packed, lanes + 32)], axis=0)
                put(base + ROWS + EDGE * k, main, halo)
        along = dot(source[...], ra_both_ref[...]) + dot(
            source[:, : 2 * LANES], ra_low_ref[...]
        )
        for j in range(batch):
            pair = step * (batch // 2) + j // 2
            rows = along[j * SPAN : (j + 1) * SPAN]
            for s in range(3):
                high, low = split(rows[:, s * LANES : (s + 1) * LANES])
                lanes = slice((j % 2) * LANES, (j % 2 + 1) * LANES)
                ra_done[s, pair, :SPAN, lanes] = high
                ra_done[s, pair, SPAN:, lanes] = low
            c = step * batch + j
            tile, slot = c // half_c, c % half_c
            edges[tile] = edges[tile] + pltpu.roll(rows[:, 3 * LANES :], 2 * slot, 1)
        return carry

    lax.fori_loop(0, channels // batch, smooth_ra, 0)

    beside = jnp.concatenate([edges[0], edges[1]], axis=1)
    beside = jnp.concatenate(split(beside), axis=0)
    which = lane_index((OUT, 2 * LANES)) % LANES // 32
    smoothed = jnp.zeros((OUT, 2 * LANES), jnp.float32)
    for s in range(3):
        both = dot(dec_ref[s], beside)
        smoothed = jnp.where(which == s, both[:OUT] + both[OUT:], smoothed)
    smoothed = split(smoothed)
    beside_squares = []
    for b in range(2):
        summed = dot(smoothed[0], box_ref[b]) + dot(smoothed[1], box_ref[b])
        square = split(summed * summed)
        beside_squares.append(
            [dot(square[0], gather_ref[s]) + dot(square[1], gather_ref[s]) for s in range(3)]
        )

    lane = lane_index((OUT, LANES))
    row = lax.broadcasted_iota(jnp.int32, (OUT, LANES), 0)
    outside = ((row == ROWS) & (dec_at == 0)) | ((row == ROWS + 1) & (dec_at == dec_n - 1))
    no_side = ((lane == 0) & (ra_at == 0)) | ((lane == LANES - 1) & (ra_at == ra_n - 1))

    copies = []
    for s in range(3):
        def smooth_dec(pair, carry):
            both = dot(dec_ref[s], ra_done[s, pair])
            both = both[:OUT] + both[OUT:]
            smooth[3 + 2 * pair] = both[:, :LANES]
            smooth[4 + 2 * pair] = both[:, LANES:]
            return carry

        for k in range(3):
            smooth[k] = jnp.zeros((OUT, LANES), jnp.float32)
            smooth[3 + channels + k] = jnp.zeros((OUT, LANES), jnp.float32)
        lax.fori_loop(0, channels // 2, smooth_dec, 0, unroll=4)

        def sum_up(c, squares):
            triple = smooth[c + 2] + smooth[c + 3] + smooth[c + 4]
            wide = triple + (smooth[c] + smooth[c + 1]) + (smooth[c + 5] + smooth[c + 6])
            result[2 * s, c] = triple[:ROWS]
            result[2 * s + 1, c] = wide[:ROWS]
            return squares[0] + triple * triple, squares[1] + wide * wide

        zero = jnp.zeros((OUT, LANES), jnp.float32)
        squares = lax.fori_loop(0, channels, sum_up, (zero, zero), unroll=4)
        for b, width in enumerate(boxcar_widths):
            square = jnp.where(outside, 0.0, squares[b])
            beside_square = jnp.where(no_side | outside, 0.0, beside_squares[b][s])
            across = square + beside_square
            across = across + jnp.where(lane == 0, 0.0, pltpu.roll(square, 1, 1))
            across = across + jnp.where(lane == LANES - 1, 0.0, pltpu.roll(square, LANES - 1, 1))
            framed[8 : 8 + ROWS] = across[:ROWS]
            framed[7:8] = across[ROWS : ROWS + 1]
            framed[8 + ROWS : 9 + ROWS] = across[ROWS + 1 : ROWS + 2]
            boxed = framed[7 : 7 + ROWS] + framed[8 : 8 + ROWS] + framed[9 : 9 + ROWS]
            scale = 1.0 / jnp.sqrt(boxed / (9.0 * channels) + width * width * epsilon)

            def normalize(c, carry):
                result[2 * s + b, c] = result[2 * s + b, c] * scale
                return carry

            lax.fori_loop(0, channels, normalize, 0, unroll=4)
            copy = pltpu.make_async_copy(result.at[2 * s + b], out_ref.at[s, b], sems.at[2 * s + b])
            copy.start()
            copies.append(copy)
    for copy in copies:
        copy.wait()


def local(cube):
    tiles = lax.axis_size("ra")
    vmem = pl.BlockSpec(memory_space=pltpu.VMEM)
    f32 = jnp.float32
    channels = tiles
    chunks = pl.pallas_call(
        pack_kernel,
        out_shape=jax.ShapeDtypeStruct((tiles, CHUNK, LANES), f32),
        in_specs=[vmem],
        out_specs=vmem,
        compiler_params=pltpu.CompilerParams(vmem_limit_bytes=32 * 2**20),
        name="pack",
    )(cube)
    tile = lax.all_to_all(chunks, "ra", split_axis=0, concat_axis=0, tiled=True)
    edge = jax.ShapeDtypeStruct((channels * (EDGE + 4), LANES), f32)
    top, bottom = pl.pallas_call(
        edge_kernel,
        out_shape=(edge, edge),
        in_specs=[vmem],
        out_specs=(vmem, vmem),
        compiler_params=pltpu.CompilerParams(vmem_limit_bytes=32 * 2**20),
        name="edges",
    )(tile)
    count = lax.axis_size("dec")
    down = [(i, i + 1) for i in range(count - 1)]
    up = [(i + 1, i) for i in range(count - 1)]
    above = lax.ppermute(bottom, "dec", down)
    below = lax.ppermute(top, "dec", up)
    batch = 8
    ra_both, ra_low = ra_weights()
    box, gather = edge_weights(channels)
    return pl.pallas_call(
        functools.partial(snr_kernel, batch=batch),
        out_shape=jax.ShapeDtypeStruct((3, 2, channels, ROWS, LANES), f32),
        in_specs=[vmem] * 8,
        out_specs=pl.BlockSpec(memory_space=pl.ANY),
        scratch_shapes=[
            pltpu.VMEM((batch * SPAN, 4 * LANES), jnp.bfloat16),
            pltpu.VMEM((3, channels // 2, 2 * SPAN, 2 * LANES), jnp.bfloat16),
            pltpu.VMEM((channels + 6, OUT, LANES), f32),
            pltpu.VMEM((6, channels, ROWS, LANES), f32),
            pltpu.VMEM((2, SPAN, LANES), f32),
            pltpu.VMEM((ROWS + 16, LANES), f32),
            pltpu.SemaphoreType.DMA((6,)),
        ],
        compiler_params=pltpu.CompilerParams(vmem_limit_bytes=48 * 2**20),
        name="snr",
    )(
        tile, above, below,
        jnp.asarray(ra_both), jnp.asarray(ra_low), jnp.asarray(dec_weights()),
        jnp.asarray(box), jnp.asarray(gather),
    )


def solution(mesh):
    return jax.shard_map(
        local,
        mesh=mesh,
        in_specs=(P("ra", "dec", None),),
        out_specs=P(None, None, None, "dec", "ra"),
        check_vma=False,
    )
```

```python
import functools

import jax
import jax.numpy as jnp
import ml_dtypes
import numpy as np
from jax import lax
from jax.experimental import pallas as pl
from jax.experimental.pallas import tpu as pltpu
from jax.sharding import PartitionSpec as P

sigma_values = (1, 2, 4)
boxcar_widths = (3, 7)
epsilon = 1e-06

LANES = 128
ROWS = 64
EDGE = 16
OUT = 40
HALF = 40
CHUNK = 2 * HALF
edge_rows = tuple(range(0, EDGE)) + tuple(range(ROWS - EDGE, ROWS))
middle_rows = tuple(range(EDGE, ROWS - EDGE))
tile_rows = edge_rows + middle_rows
halo_rows = tuple(range(-EDGE, 0)) + tuple(range(ROWS, ROWS + EDGE))
inner_out = middle_rows + (EDGE - 1, ROWS - EDGE)
outer_out = edge_rows + (-1, EDGE, ROWS - EDGE - 1, ROWS)
inner_runs = ((0, 32, 32, 33),)
outer_runs = ((0, 16, 32, 33), (16, 16, 34, 35))
beside_cols = np.array(tuple(range(LANES, LANES + 16)) + tuple(range(-16, 0)))


def taps(distance, sigma):
    reach = 3 * sigma
    lags = np.arange(-reach, reach + 1, dtype=np.float64)
    weight_sum = np.sum(np.exp(-lags * lags / (2.0 * sigma * sigma)))
    value = np.exp(-(distance.astype(np.float64) ** 2) / (2.0 * sigma * sigma)) / weight_sum
    return np.where(np.abs(distance) <= reach, value, 0.0).astype(np.float32)


def halves(value):
    high = value.astype(ml_dtypes.bfloat16)
    low = (value - high.astype(np.float32)).astype(ml_dtypes.bfloat16)
    return high, low


def ra_weights():
    def band(cols):
        weights = np.zeros((len(cols), 4 * LANES), np.float32)
        for s, sigma in enumerate(sigma_values):
            weights[:, s * LANES : (s + 1) * LANES] = taps(
                cols[:, None] - np.arange(LANES)[None, :], sigma
            )
            for side, col in enumerate((-1, LANES)):
                weights[:, 3 * LANES + 32 * s + side] = taps(cols - col, sigma)
        return halves(weights)

    high, low = band(np.arange(LANES))
    beside_high, beside_low = band(beside_cols)
    nothing = np.zeros_like(beside_high)
    parts = [high, high, low, beside_high, beside_high, beside_low, nothing]
    return np.concatenate(parts, axis=0)


def dec_weights(out_rows, in_rows):
    result = np.zeros((3, 2 * OUT, 2 * len(in_rows)), ml_dtypes.bfloat16)
    for s, sigma in enumerate(sigma_values):
        weights = taps(np.array(in_rows)[None, :] - np.array(out_rows)[:, None], sigma)
        high, low = halves(weights)
        result[s, : len(out_rows), : len(in_rows)] = high
        result[s, : len(out_rows), len(in_rows) :] = high
        result[s, OUT : OUT + len(out_rows), : len(in_rows)] = low
    return result


def edge_weights(channels):
    half = channels // 2
    lane = np.arange(2 * LANES)
    tile, within = lane // LANES, lane % LANES
    sigma, slot = within // 32, within % 32
    channel, side = tile * half + slot // 2, slot % 2
    used = (sigma < 3) & (slot < 2 * half)
    same = used[:, None] & used[None, :] & (sigma[:, None] == sigma[None, :])
    same &= side[:, None] == side[None, :]
    boxcars = [
        same & (np.abs(channel[:, None] - channel[None, :]) <= width // 2)
        for width in boxcar_widths
    ]
    gathers = np.zeros((3, 2 * LANES, LANES), bool)
    for s in range(3):
        gathers[s, :, 0] = used & (sigma == s) & (side == 0)
        gathers[s, :, LANES - 1] = used & (sigma == s) & (side == 1)
    return (
        np.stack(boxcars).astype(ml_dtypes.bfloat16),
        gathers.astype(ml_dtypes.bfloat16),
    )


def lane_index(shape):
    return lax.broadcasted_iota(jnp.int32, shape, len(shape) - 1)


def split(value):
    high = value.astype(jnp.bfloat16)
    low = (value - high.astype(jnp.float32)).astype(jnp.bfloat16)
    return high, low


def dot(a, b):
    return jnp.dot(a, b, preferred_element_type=jnp.float32)


def pack_rows(block, out_ref, tile, at):
    lane = lane_index((8, LANES))
    here, right, left = block
    packed = jnp.zeros((8, LANES), jnp.float32)
    for group in range(4):
        out_ref[tile, at + 8 * group : at + 8 * group + 8, :] = here(group)
        first, first_at = right(group)
        last, last_at = left(group)
        first = turn(first, 32 * group - first_at)
        last = turn(last, 32 * group + 16 - last_at)
        lanes = lane - 32 * group
        packed = jnp.where((lanes >= 0) & (lanes < 16), first, packed)
        packed = jnp.where((lanes >= 16) & (lanes < 32), last, packed)
    out_ref[tile, at + 32 : at + HALF, :] = packed


def turn(value, lanes):
    lanes = lanes % LANES
    return pltpu.roll(value, lanes, 1) if lanes else value


def far_half():
    return 1 - (lax.axis_index("ra") // 4) % 2


def rows_copies(cube_ref, rows, held, sems):
    copies = []
    for k, at in enumerate(range(0, len(rows), 16)):
        source = cube_ref.at[0, pl.ds(rows[at], 16), :]
        copies.append(pltpu.make_async_copy(source, held.at[pl.ds(at, 16), :], sems.at[k]))
    for copy in copies:
        copy.start()
    return copies


def column_kernel(tiles, cube_ref, far_ref, near_ref, held, sems):
    copies = rows_copies(cube_ref, edge_rows, held, sems)
    far = far_half()
    lane = lane_index((8, LANES))
    wide = tiles // 8

    def columns(tile, at):
        return held[at : at + 8, pl.ds(pl.multiple_of(tile * LANES, LANES), LANES)]

    for group in range(4):
        at = 8 * group
        if group % 2 == 0:
            copies[group // 2].wait()
        for half_z, out_ref in ((far, far_ref), (1 - far, near_ref)):
            beside = jnp.zeros((8, LANES), jnp.float32)
            for x in range(wide):
                first = 8 * x + 4 * half_z
                for y in range(4):
                    out_ref[4 * x + y, at : at + 8, :] = columns(first + y, at)
                right = turn(columns(jnp.minimum(first + 4, tiles - 1), at), 32 * x)
                left = turn(columns(jnp.maximum(first - 1, 0), at), 32 * x + 32)
                right = jnp.where(first + 4 < tiles, right, 0.0)
                left = jnp.where(first > 0, left, 0.0)
                lanes = lane - 32 * x
                beside = jnp.where((lanes >= 0) & (lanes < 16), right, beside)
                beside = jnp.where((lanes >= 16) & (lanes < 32), left, beside)
            out_ref[4 * wide, at : at + 8, :] = beside


def pack_cube(tiles, held, half_z, out_ref, at):
    def columns(tile, group):
        inside = (tile >= 0) & (tile < tiles)
        tile = jnp.clip(tile, 0, tiles - 1)
        lanes = pl.ds(pl.multiple_of(tile * LANES, LANES), LANES)
        return inside, held[8 * group : 8 * group + 8, lanes]

    for x in range(tiles // 8):
        for y in range(4):
            tile = 8 * x + 4 * half_z + y

            def here(group):
                return columns(tile, group)[1]

            def right(group):
                inside, value = columns(tile + 1, group)
                return (jnp.where(inside, value, 0.0) if y == 3 else value), 0

            def left(group):
                inside, value = columns(tile - 1, group)
                return (jnp.where(inside, value, 0.0) if y == 0 else value), LANES - 16

            pack_rows((here, right, left), out_ref, 4 * x + y, at)


def middle_kernel(tiles, cube_ref, out_ref, held, sems):
    for copy in rows_copies(cube_ref, middle_rows, held, sems):
        copy.wait()
    far = far_half()
    pack_cube(tiles, held, far, out_ref, 0)
    pack_cube(tiles, held, 1 - far, out_ref, HALF)


def edge_rows_kernel(after_ref, far_ref, near_ref, out_ref):
    del after_ref
    wide = out_ref.shape[0] // 4
    for start, ref in ((0, far_ref), (HALF, near_ref)):
        for x in range(wide):
            for y in range(4):
                tile = 4 * x + y

                def here(group):
                    return ref[tile, 8 * group : 8 * group + 8, :]

                def right(group):
                    if y < 3:
                        return ref[tile + 1, 8 * group : 8 * group + 8, :], 0
                    return ref[4 * wide, 8 * group : 8 * group + 8, :], 32 * x

                def left(group):
                    if y > 0:
                        return ref[tile - 1, 8 * group : 8 * group + 8, :], LANES - 16
                    return ref[4 * wide, 8 * group : 8 * group + 8, :], 32 * x + 16

                pack_rows((here, right, left), out_ref, tile, start)


def edge_kernel(edge_ref, top_ref, bottom_ref):
    count = edge_ref.shape[0]
    channels = 2 * count
    lane = lane_index((8, LANES))
    for part, start in enumerate((HALF, 0)):
        for i in range(count):
            at = (part * count + i) * EDGE
            top_ref[at : at + EDGE, :] = edge_ref[i, start : start + EDGE, :]
            bottom_ref[at : at + EDGE, :] = edge_ref[i, start + EDGE : start + 2 * EDGE, :]
        for pair in range(count // 2):
            at = channels * EDGE + 8 * (part * count // 2 + pair)
            first = edge_ref[2 * pair, start + 32 : start + HALF, :]
            second = edge_ref[2 * pair + 1, start + 32 : start + HALF, :]
            top_ref[at : at + 8, :] = jnp.where(lane < 64, first, pltpu.roll(second, 64, 1))
            bottom_ref[at : at + 8, :] = jnp.where(lane < 64, pltpu.roll(first, 64, 1), second)


def put_rows(source, at, main, packed, places):
    lane = lane_index((8, LANES))
    high, low = split(main)
    beside = []
    for value, place in zip(packed, places):
        value_high = value.astype(jnp.bfloat16).astype(jnp.float32)
        value_low = value - value_high
        mix = jnp.where(lane < 64, turn(value_low, 32 - place), turn(value_high, 64 - place))
        mix = jnp.where(lane < 32, turn(value_high, -place), mix)
        beside.append(jnp.where(lane < 96, mix, 0.0))
    source[at : at + 16, :LANES] = low
    source[at : at + 16, LANES : 2 * LANES] = high
    source[at : at + 16, 2 * LANES :] = jnp.concatenate(beside, axis=0).astype(jnp.bfloat16)


def smooth_ra(source, weights_ref, rows, pairs, channels_at, done, edges):
    operand = jnp.concatenate([source[:, : 2 * LANES], source[:, LANES:]], axis=1)
    along = dot(operand, weights_ref[...])
    half = done.shape[1]
    for j, (pair, c) in enumerate(zip(pairs, channels_at)):
        block = along[j * rows : (j + 1) * rows]
        lanes = slice((j % 2) * LANES, (j % 2 + 1) * LANES)
        for s in range(3):
            high, low = split(block[:, s * LANES : (s + 1) * LANES])
            done[s, pair, :rows, lanes] = high
            done[s, pair, rows:, lanes] = low
        tile, slot = c // half, c % half
        edges[tile] = edges[tile] + pltpu.roll(block[:, 3 * LANES :], 2 * slot, 1)


def smooth_dec(parts, s, pair):
    both = sum(dot(weights[s], done[s, pair]) for weights, done in parts)
    return both[:OUT] + both[OUT:]


def beside_squares(parts, box_ref, gather_ref):
    which = lane_index((OUT, 2 * LANES)) % LANES // 32
    smoothed = jnp.zeros((OUT, 2 * LANES), jnp.float32)
    parts = [
        (weights, jnp.concatenate(split(jnp.concatenate([edges[0], edges[1]], axis=1)), axis=0))
        for weights, edges in parts
    ]
    for s in range(3):
        both = sum(dot(weights[s], value) for weights, value in parts)
        smoothed = jnp.where(which == s, both[:OUT] + both[OUT:], smoothed)
    smoothed = split(smoothed)
    result = []
    for b in range(2):
        summed = dot(smoothed[0], box_ref[b]) + dot(smoothed[1], box_ref[b])
        square = split(summed * summed)
        result.append(
            [dot(square[0], gather_ref[s]) + dot(square[1], gather_ref[s]) for s in range(3)]
        )
    return result


def snr_rows(parts, beside, outside, runs, targets, smooth, result, framed, sems):
    channels = result.shape[1]
    ra_at, ra_n = lax.axis_index("ra"), lax.axis_size("ra")
    lane = lane_index((OUT, LANES))
    row = lax.broadcasted_iota(jnp.int32, (OUT, LANES), 0)
    gone = row < 0
    for at, condition in outside:
        gone = gone | ((row == at) & condition)
    no_side = ((lane == 0) & (ra_at == 0)) | ((lane == LANES - 1) & (ra_at == ra_n - 1))
    rows = sum(run[1] for run in runs)
    copies = []
    for s in range(3):

        def smooth_pair(pair, carry):
            both = smooth_dec(parts, s, pair)
            smooth[3 + 2 * pair] = both[:, :LANES]
            smooth[4 + 2 * pair] = both[:, LANES:]
            return carry

        for k in range(3):
            smooth[k] = jnp.zeros((OUT, LANES), jnp.float32)
            smooth[3 + channels + k] = jnp.zeros((OUT, LANES), jnp.float32)
        lax.fori_loop(0, channels // 2, smooth_pair, 0, unroll=4)

        squares = [[], []]
        for at in range(0, OUT, 8):
            planes = [smooth[k, at : at + 8, :] for k in range(channels + 6)]
            triples = [planes[k] + planes[k + 1] + planes[k + 2] for k in range(channels + 4)]
            totals = [[None, None], [None, None]]
            for c in range(channels):
                wide = triples[c] + triples[c + 3] + planes[c + 6]
                for b, value in enumerate((triples[c + 2], wide)):
                    if at < rows:
                        result[2 * s + b, c, at : at + 8, :] = value
                    square = value * value
                    total = totals[b][c % 2]
                    totals[b][c % 2] = square if total is None else total + square
            for b in range(2):
                squares[b].append(totals[b][0] + totals[b][1])
        for b, width in enumerate(boxcar_widths):
            square = jnp.where(gone, 0.0, jnp.concatenate(squares[b], axis=0))
            across = square + jnp.where(no_side | gone, 0.0, beside[b][s])
            across = across + jnp.where(lane == 0, 0.0, pltpu.roll(square, 1, 1))
            across = across + jnp.where(lane == LANES - 1, 0.0, pltpu.roll(square, LANES - 1, 1))
            boxed = []
            at = 0
            for first, length, before, after in runs:
                at = at + 8
                framed[at : at + length] = across[first : first + length]
                framed[at - 1 : at] = across[before : before + 1]
                framed[at + length : at + length + 1] = across[after : after + 1]
                boxed.append(
                    framed[at - 1 : at - 1 + length]
                    + framed[at : at + length]
                    + framed[at + 1 : at + 1 + length]
                )
                at = at + length + 8
            boxed = jnp.concatenate(boxed, axis=0) if len(boxed) > 1 else boxed[0]
            scale = 1.0 / jnp.sqrt(boxed / (9.0 * channels) + width * width * epsilon)

            def normalize(c, carry):
                result[2 * s + b, c] = result[2 * s + b, c] * scale
                return carry

            lax.fori_loop(0, channels, normalize, 0, unroll=8)
            for k, (first, length, _, _) in enumerate(runs):
                copy = pltpu.make_async_copy(
                    result.at[2 * s + b, :, pl.ds(first, length), :],
                    targets(s, b)[k],
                    sems.at[len(runs) * (2 * s + b) + k],
                )
                copy.start()
                copies.append(copy)
    for copy in copies:
        copy.wait()


def inner_kernel(
    edge_ref, middle_ref, far_middle_ref, ra_ref, dec_ref, box_ref, gather_ref,
    out_ref, done_ref, edges_ref,
    source, smooth, result, framed, sems,
    *, batch,
):
    channels = 2 * edge_ref.shape[0]
    near = (lax.axis_index("ra") // 4) % 2
    edges_ref[...] = jnp.zeros_like(edges_ref)
    halves_of = ((edge_ref, HALF), (middle_ref, HALF)), ((edge_ref, 0), (far_middle_ref, 0))
    for part, parts in enumerate(halves_of):
        half_z = near if part == 0 else 1 - near
        for step in range(channels // 2 // batch):
            pairs, channels_at = [], []
            for j in range(batch):
                i = step * batch + j
                for half, (ref, at) in enumerate(parts):
                    packed = ref[i, at + 32 : at + HALF, :]
                    for k in range(2):
                        main = ref[i, at + 16 * k : at + 16 * k + 16, :]
                        put_rows(
                            source.at[part], j * ROWS + 32 * half + 16 * k, main,
                            (packed, packed), (64 * k, 64 * k + 32),
                        )
                pairs.append(4 * (i // 4) + 2 * half_z + (i % 4) // 2)
                channels_at.append(8 * (i // 4) + 4 * half_z + i % 4)
            smooth_ra(source.at[part], ra_ref, ROWS, pairs, channels_at, done_ref, edges_ref)
    beside = beside_squares([(dec_ref, edges_ref)], box_ref, gather_ref)

    def targets(s, b):
        return [out_ref.at[s, b, :, pl.ds(EDGE, ROWS - 2 * EDGE), :]]

    snr_rows(
        [(dec_ref, done_ref)], beside, (), inner_runs, targets, smooth, result, framed, sems
    )


def outer_kernel(
    held_ref, above_ref, below_ref, done_ref, edges_ref,
    ra_ref, dec_ref, dec_halo_ref, box_ref, gather_ref,
    out_ref,
    source, halo_done, halo_edges, smooth, result, framed, sems,
    *, batch,
):
    del held_ref
    channels = 2 * done_ref.shape[1]
    near = (lax.axis_index("ra") // 4) % 2
    dec_at, dec_n = lax.axis_index("dec"), lax.axis_size("dec")
    halo_edges[...] = jnp.zeros_like(halo_edges)
    for step in range(channels // batch):
        pairs, channels_at = [], []
        for j in range(batch):
            at = step * batch + j
            part, i = at // (channels // 2), at % (channels // 2)
            for k, ref in enumerate((above_ref, below_ref)):
                row = channels * EDGE + 8 * (at // 2)
                packed = ref[row : row + 8, :]
                lanes = 64 * (at % 2)
                put_rows(
                    source.at[step % 2], 2 * EDGE * j + EDGE * k, ref[at * EDGE : (at + 1) * EDGE, :],
                    (packed, packed), (lanes, lanes + 32),
                )
            half_z = near if part == 0 else 1 - near
            pairs.append(4 * (i // 4) + 2 * half_z + (i % 4) // 2)
            channels_at.append(8 * (i // 4) + 4 * half_z + i % 4)
        smooth_ra(
            source.at[step % 2], ra_ref, 2 * EDGE, pairs, channels_at, halo_done, halo_edges
        )
    parts = [(dec_ref, done_ref), (dec_halo_ref, halo_done)]
    beside = beside_squares(
        [(dec_ref, edges_ref), (dec_halo_ref, halo_edges)], box_ref, gather_ref
    )

    def targets(s, b):
        return [out_ref.at[s, b, :, pl.ds(at, EDGE), :] for at in (0, ROWS - EDGE)]

    outside = ((32, dec_at == 0), (35, dec_at == dec_n - 1))
    snr_rows(parts, beside, outside, outer_runs, targets, smooth, result, framed, sems)


def local(cube):
    tiles = channels = lax.axis_size("ra")
    vmem = pl.BlockSpec(memory_space=pltpu.VMEM)
    f32 = jnp.float32

    def call(kernel, shapes, operands, name, outside=(), scratch=()):
        return pl.pallas_call(
            kernel,
            out_shape=shapes,
            in_specs=[pl.BlockSpec(memory_space=pl.ANY)] * len(outside) + [vmem] * len(operands),
            out_specs=jax.tree.map(lambda _: vmem, shapes),
            scratch_shapes=scratch,
            compiler_params=pltpu.CompilerParams(vmem_limit_bytes=32 * 2**20),
            name=name,
        )(*outside, *operands)

    across = [(i, i ^ 4) for i in range(tiles)]
    groups = [[8 * x + 4 * z + y for x in range(tiles // 8) for y in range(4)] for z in range(2)]

    def regroup(chunks):
        return lax.all_to_all(
            chunks, "ra", split_axis=0, concat_axis=0, tiled=True, axis_index_groups=groups
        )

    part = jax.ShapeDtypeStruct((tiles // 2 + 1, 32, LANES), f32)
    chunk = jax.ShapeDtypeStruct((tiles // 2, CHUNK, LANES), f32)
    rows = [pltpu.VMEM((32, cube.shape[2]), f32), pltpu.SemaphoreType.DMA((2,))]
    columns = functools.partial(column_kernel, tiles)
    part, near_part = call(columns, (part, part), (), "columns", (cube,), rows)
    part = lax.ppermute(part, "ra", across)

    def regroup_middle(cube):
        chunks = call(functools.partial(middle_kernel, tiles), chunk, (), "middle", (cube,), rows)
        return regroup(chunks)

    def nothing(cube):
        return jnp.zeros(chunk.shape, f32)

    middle = lax.cond(lax.axis_index("ra") >= 0, regroup_middle, nothing, cube)
    far_middle = lax.ppermute(middle[:, :HALF], "ra", across)
    edge = call(edge_rows_kernel, chunk, (part, near_part), "edge_rows", (middle,))
    edge_chunk = regroup(edge)
    edge = jax.ShapeDtypeStruct((channels * (EDGE + 4), LANES), f32)
    top, bottom = call(edge_kernel, (edge, edge), (edge_chunk,), "edges")
    count = lax.axis_size("dec")
    down = [(i, i + 1) for i in range(count - 1)]
    up = [(i + 1, i) for i in range(count - 1)]
    above = lax.ppermute(bottom, "dec", down)
    below = lax.ppermute(top, "dec", up)
    box, gather = (jnp.asarray(value) for value in edge_weights(channels))
    along = jnp.asarray(ra_weights())
    anywhere = pl.BlockSpec(memory_space=pl.ANY)
    out = jax.ShapeDtypeStruct((3, 2, channels, ROWS, LANES), f32)
    batch = 8
    work = [
        pltpu.VMEM((channels + 6, OUT, LANES), f32),
        pltpu.VMEM((6, channels, 2 * EDGE, LANES), f32),
        pltpu.VMEM((ROWS + 16, LANES), f32),
    ]
    params = pltpu.CompilerParams(vmem_limit_bytes=32 * 2**20)
    held, done, edges = pl.pallas_call(
        functools.partial(inner_kernel, batch=batch),
        out_shape=(
            out,
            jax.ShapeDtypeStruct((3, channels // 2, 2 * ROWS, 2 * LANES), jnp.bfloat16),
            jax.ShapeDtypeStruct((2, ROWS, LANES), f32),
        ),
        in_specs=[vmem] * 7,
        out_specs=(anywhere, vmem, vmem),
        scratch_shapes=[pltpu.VMEM((2, batch * ROWS, 3 * LANES), jnp.bfloat16)]
        + work
        + [pltpu.SemaphoreType.DMA((6,))],
        compiler_params=params,
        cost_estimate=pl.CostEstimate(
            flops=2 * 10**9, bytes_accessed=8 * 2**20, transcendentals=0
        ),
        name="inner",
    )(
        edge_chunk, middle, far_middle, along,
        jnp.asarray(dec_weights(inner_out, tile_rows)), box, gather,
    )
    batch = 16
    return pl.pallas_call(
        functools.partial(outer_kernel, batch=batch),
        out_shape=out,
        in_specs=[anywhere] + [vmem] * 9,
        out_specs=anywhere,
        scratch_shapes=[
            pltpu.VMEM((2, batch * 2 * EDGE, 3 * LANES), jnp.bfloat16),
            pltpu.VMEM((3, channels // 2, 4 * EDGE, 2 * LANES), jnp.bfloat16),
            pltpu.VMEM((2, 2 * EDGE, LANES), f32),
        ]
        + work
        + [pltpu.SemaphoreType.DMA((12,))],
        input_output_aliases={0: 0},
        compiler_params=params,
        cost_estimate=pl.CostEstimate(
            flops=10**9, bytes_accessed=8 * 2**20, transcendentals=0
        ),
        name="outer",
    )(
        held, above, below, done, edges, along,
        jnp.asarray(dec_weights(outer_out, tile_rows)),
        jnp.asarray(dec_weights(outer_out, halo_rows)), box, gather,
    )


def solution(mesh):
    return jax.shard_map(
        local,
        mesh=mesh,
        in_specs=(P("ra", "dec", None),),
        out_specs=P(None, None, None, "dec", "ra"),
        check_vma=False,
    )
```

```python
import functools

import jax
import jax.numpy as jnp
import ml_dtypes
import numpy as np
from jax import lax
from jax.experimental import pallas as pl
from jax.experimental.pallas import tpu as pltpu
from jax.sharding import PartitionSpec as P

sigma_values = (1, 2, 4)
boxcar_widths = (3, 7)
epsilon = 1e-06

LANES = 128
ROWS = 64
EDGE = 16
OUT = 40
STEP = 1024
HALF = 40
CHUNK = 2 * HALF
edge_rows = tuple(range(0, EDGE)) + tuple(range(ROWS - EDGE, ROWS))
middle_rows = tuple(range(EDGE, ROWS - EDGE))
tile_rows = edge_rows + middle_rows
halo_rows = tuple(range(-EDGE, 0)) + tuple(range(ROWS, ROWS + EDGE))
inner_out = middle_rows + (EDGE - 1, ROWS - EDGE)
outer_out = edge_rows + (-1, EDGE, ROWS - EDGE - 1, ROWS)
inner_runs = ((0, 32, 32, 33),)
outer_runs = ((0, 16, 32, 33), (16, 16, 34, 35))
beside_cols = np.array(tuple(range(LANES, LANES + 16)) + tuple(range(-16, 0)))


def taps(distance, sigma):
    reach = 3 * sigma
    lags = np.arange(-reach, reach + 1, dtype=np.float64)
    weight_sum = np.sum(np.exp(-lags * lags / (2.0 * sigma * sigma)))
    value = np.exp(-(distance.astype(np.float64) ** 2) / (2.0 * sigma * sigma)) / weight_sum
    return np.where(np.abs(distance) <= reach, value, 0.0).astype(np.float32)


def halves(value):
    high = value.astype(ml_dtypes.bfloat16)
    low = (value - high.astype(np.float32)).astype(ml_dtypes.bfloat16)
    return high, low


def ra_weights():
    def band(cols):
        weights = np.zeros((len(cols), 4 * LANES), np.float32)
        for s, sigma in enumerate(sigma_values):
            weights[:, s * LANES : (s + 1) * LANES] = taps(
                cols[:, None] - np.arange(LANES)[None, :], sigma
            )
            for side, col in enumerate((-1, LANES)):
                weights[:, 3 * LANES + 32 * s + side] = taps(cols - col, sigma)
        return halves(weights)

    high, low = band(np.arange(LANES))
    beside_high, beside_low = band(beside_cols)
    nothing = np.zeros_like(beside_high)
    parts = [high, high, low, beside_high, beside_high, beside_low, nothing]
    return np.concatenate(parts, axis=0)


def dec_weights(out_rows, in_rows):
    result = np.zeros((3, 2 * OUT, 2 * len(in_rows)), ml_dtypes.bfloat16)
    for s, sigma in enumerate(sigma_values):
        weights = taps(np.array(in_rows)[None, :] - np.array(out_rows)[:, None], sigma)
        high, low = halves(weights)
        result[s, : len(out_rows), : len(in_rows)] = high
        result[s, : len(out_rows), len(in_rows) :] = high
        result[s, OUT : OUT + len(out_rows), : len(in_rows)] = low
    return result


def edge_weights(channels):
    half = channels // 2
    lane = np.arange(2 * LANES)
    tile, within = lane // LANES, lane % LANES
    sigma, slot = within // 32, within % 32
    channel, side = tile * half + slot // 2, slot % 2
    used = (sigma < 3) & (slot < 2 * half)
    same = used[:, None] & used[None, :] & (sigma[:, None] == sigma[None, :])
    same &= side[:, None] == side[None, :]
    boxcars = [
        same & (np.abs(channel[:, None] - channel[None, :]) <= width // 2)
        for width in boxcar_widths
    ]
    gathers = np.zeros((3, 2 * LANES, LANES), bool)
    for s in range(3):
        gathers[s, :, 0] = used & (sigma == s) & (side == 0)
        gathers[s, :, LANES - 1] = used & (sigma == s) & (side == 1)
    return (
        np.concatenate(boxcars, axis=1).astype(ml_dtypes.bfloat16),
        np.concatenate(gathers, axis=1).astype(ml_dtypes.bfloat16),
    )


def lane_index(shape):
    return lax.broadcasted_iota(jnp.int32, shape, len(shape) - 1)


def split(value):
    high = value.astype(jnp.bfloat16)
    low = (value - high.astype(jnp.float32)).astype(jnp.bfloat16)
    return high, low


def dot(a, b):
    return jnp.dot(a, b, preferred_element_type=jnp.float32)


def pack_rows(block, out_ref, tile, at):
    lane = lane_index((8, LANES))
    here, right, left = block
    packed = jnp.zeros((8, LANES), jnp.float32)
    for group in range(4):
        out_ref[tile, at + 8 * group : at + 8 * group + 8, :] = here(group)
        first, first_at = right(group)
        last, last_at = left(group)
        first = turn(first, 32 * group - first_at)
        last = turn(last, 32 * group + 16 - last_at)
        lanes = lane - 32 * group
        packed = jnp.where((lanes >= 0) & (lanes < 16), first, packed)
        packed = jnp.where((lanes >= 16) & (lanes < 32), last, packed)
    out_ref[tile, at + 32 : at + HALF, :] = packed


def turn(value, lanes):
    lanes = lanes % LANES
    return pltpu.roll(value, lanes, 1) if lanes else value


def far_half():
    return 1 - (lax.axis_index("ra") // 4) % 2


def rows_copies(cube_ref, rows, held, sems):
    copies = []
    for k, at in enumerate(range(0, len(rows), 16)):
        source = cube_ref.at[0, pl.ds(rows[at], 16), :]
        copies.append(pltpu.make_async_copy(source, held.at[pl.ds(at, 16), :], sems.at[k]))
    for copy in copies:
        copy.start()
    return copies


def column_kernel(tiles, cube_ref, far_ref, near_ref, held, sems):
    copies = rows_copies(cube_ref, edge_rows, held, sems)
    far = far_half()
    lane = lane_index((8, LANES))
    wide = tiles // 8

    def columns(tile, at):
        return held[at : at + 8, pl.ds(pl.multiple_of(tile * LANES, LANES), LANES)]

    for group in range(4):
        at = 8 * group
        if group % 2 == 0:
            copies[group // 2].wait()
        for half_z, out_ref in ((far, far_ref), (1 - far, near_ref)):
            beside = jnp.zeros((8, LANES), jnp.float32)
            for x in range(wide):
                first = 8 * x + 4 * half_z
                for y in range(4):
                    out_ref[4 * x + y, at : at + 8, :] = columns(first + y, at)
                right = turn(columns(jnp.minimum(first + 4, tiles - 1), at), 32 * x)
                left = turn(columns(jnp.maximum(first - 1, 0), at), 32 * x + 32)
                right = jnp.where(first + 4 < tiles, right, 0.0)
                left = jnp.where(first > 0, left, 0.0)
                lanes = lane - 32 * x
                beside = jnp.where((lanes >= 0) & (lanes < 16), right, beside)
                beside = jnp.where((lanes >= 16) & (lanes < 32), left, beside)
            out_ref[4 * wide, at : at + 8, :] = beside


def pack_cube(tiles, held, half_z, out_ref, at):
    def columns(tile, group):
        inside = (tile >= 0) & (tile < tiles)
        tile = jnp.clip(tile, 0, tiles - 1)
        lanes = pl.ds(pl.multiple_of(tile * LANES, LANES), LANES)
        return inside, held[8 * group : 8 * group + 8, lanes]

    for x in range(tiles // 8):
        for y in range(4):
            tile = 8 * x + 4 * half_z + y

            def here(group):
                return columns(tile, group)[1]

            def right(group):
                inside, value = columns(tile + 1, group)
                return (jnp.where(inside, value, 0.0) if y == 3 else value), 0

            def left(group):
                inside, value = columns(tile - 1, group)
                return (jnp.where(inside, value, 0.0) if y == 0 else value), LANES - 16

            pack_rows((here, right, left), out_ref, 4 * x + y, at)


def middle_kernel(tiles, cube_ref, out_ref, held, sems):
    for copy in rows_copies(cube_ref, middle_rows, held, sems):
        copy.wait()
    far = far_half()
    pack_cube(tiles, held, far, out_ref, 0)
    pack_cube(tiles, held, 1 - far, out_ref, HALF)


def edge_rows_kernel(after_ref, far_ref, near_ref, out_ref):
    del after_ref
    wide = out_ref.shape[0] // 4
    for start, ref in ((0, far_ref), (HALF, near_ref)):
        for x in range(wide):
            for y in range(4):
                tile = 4 * x + y

                def here(group):
                    return ref[tile, 8 * group : 8 * group + 8, :]

                def right(group):
                    if y < 3:
                        return ref[tile + 1, 8 * group : 8 * group + 8, :], 0
                    return ref[4 * wide, 8 * group : 8 * group + 8, :], 32 * x

                def left(group):
                    if y > 0:
                        return ref[tile - 1, 8 * group : 8 * group + 8, :], LANES - 16
                    return ref[4 * wide, 8 * group : 8 * group + 8, :], 32 * x + 16

                pack_rows((here, right, left), out_ref, tile, start)


def edge_kernel(edge_ref, top_ref, bottom_ref):
    count = edge_ref.shape[0]
    channels = 2 * count
    lane = lane_index((8, LANES))
    for part, start in enumerate((HALF, 0)):
        for i in range(count):
            at = (part * count + i) * EDGE
            top_ref[at : at + EDGE, :] = edge_ref[i, start : start + EDGE, :]
            bottom_ref[at : at + EDGE, :] = edge_ref[i, start + EDGE : start + 2 * EDGE, :]
        for pair in range(count // 2):
            at = channels * EDGE + 8 * (part * count // 2 + pair)
            first = edge_ref[2 * pair, start + 32 : start + HALF, :]
            second = edge_ref[2 * pair + 1, start + 32 : start + HALF, :]
            top_ref[at : at + 8, :] = jnp.where(lane < 64, first, pltpu.roll(second, 64, 1))
            bottom_ref[at : at + 8, :] = jnp.where(lane < 64, pltpu.roll(first, 64, 1), second)


def put_rows(source, at, main, packed, places):
    lane = lane_index((8, LANES))
    high, low = split(main)
    beside = []
    for value, place in zip(packed, places):
        value_high = value.astype(jnp.bfloat16).astype(jnp.float32)
        value_low = value - value_high
        mix = jnp.where(lane < 64, turn(value_low, 32 - place), turn(value_high, 64 - place))
        mix = jnp.where(lane < 32, turn(value_high, -place), mix)
        beside.append(jnp.where(lane < 96, mix, 0.0))
    source[at : at + 16, :LANES] = low
    source[at : at + 16, LANES : 2 * LANES] = high
    source[at : at + 16, 2 * LANES :] = jnp.concatenate(beside, axis=0).astype(jnp.bfloat16)


def smooth_ra(source, weights_ref, rows, channels_at, done, edges):
    operand = jnp.concatenate([source[:, : 2 * LANES], source[:, LANES:]], axis=1)
    along = dot(operand, weights_ref[...])
    half = done.shape[2] // LANES // 2
    for j, c in enumerate(channels_at):
        block = along[j * rows : (j + 1) * rows]
        lanes = pl.ds(pl.multiple_of(c * LANES, LANES), LANES)
        for s in range(3):
            high, low = split(block[:, s * LANES : (s + 1) * LANES])
            done[s, :rows, lanes] = high
            done[s, rows:, lanes] = low
        tile, slot = c // half, c % half
        edges[tile] = edges[tile] + pltpu.roll(block[:, 3 * LANES :], 2 * slot, 1)


def smooth_dec(parts, s, out):
    for at in range(0, out.shape[1], STEP):
        both = sum(dot(weights[s], done[s, :, at : at + STEP]) for weights, done in parts)
        out[:, at : at + STEP] = both[:OUT] + both[OUT:]


def beside_squares(parts, box_ref, gather_ref):
    which = lane_index((OUT, 2 * LANES)) % LANES // 32
    smoothed = jnp.zeros((OUT, 2 * LANES), jnp.float32)
    parts = [
        (weights, jnp.concatenate(split(jnp.concatenate([edges[0], edges[1]], axis=1)), axis=0))
        for weights, edges in parts
    ]
    for s in range(3):
        both = sum(dot(weights[s], value) for weights, value in parts)
        smoothed = jnp.where(which == s, both[:OUT] + both[OUT:], smoothed)
    high, low = split(smoothed)
    summed = dot(high, box_ref[...]) + dot(low, box_ref[...])
    summed = jnp.concatenate([summed[:, : 2 * LANES], summed[:, 2 * LANES :]], axis=0)
    high, low = split(summed * summed)
    squares = dot(high, gather_ref[...]) + dot(low, gather_ref[...])
    return [
        [squares[b * OUT : (b + 1) * OUT, s * LANES : (s + 1) * LANES] for s in range(3)]
        for b in range(2)
    ]


def boxcar_sums(smooth, rows, result):
    channels = result.shape[1]
    squares = [[], []]
    for at in range(0, OUT, 8):
        planes = {
            c: smooth[at : at + 8, c * LANES : (c + 1) * LANES] for c in range(channels)
        }

        def total(places):
            return functools.reduce(jnp.add, [planes[c] for c in places if c in planes])

        triples = {c: total(range(c - 1, c + 2)) for c in range(-1, channels + 1)}
        totals = [[None, None], [None, None]]
        for c in range(channels):
            terms = [triples[c - 2]] if c >= 1 else []
            terms += [triples[c + 1]] + ([planes[c + 3]] if c + 3 < channels else [])
            for b, value in enumerate((triples[c], functools.reduce(jnp.add, terms))):
                if at < rows:
                    result[b, c, at : at + 8, :] = value
                square = value * value
                before = totals[b][c % 2]
                totals[b][c % 2] = square if before is None else before + square
        for b in range(2):
            squares[b].append(totals[b][0] + totals[b][1])
    return [jnp.concatenate(square, axis=0) for square in squares]


def snr_rows(parts, beside, outside, runs, targets, smooth, result, framed, sems):
    channels = result.shape[1]
    ra_at, ra_n = lax.axis_index("ra"), lax.axis_size("ra")
    lane = lane_index((OUT, LANES))
    row = lax.broadcasted_iota(jnp.int32, (OUT, LANES), 0)
    gone = row < 0
    for at, condition in outside:
        gone = gone | ((row == at) & condition)
    no_side = ((lane == 0) & (ra_at == 0)) | ((lane == LANES - 1) & (ra_at == ra_n - 1))
    rows = sum(run[1] for run in runs)
    copies = []
    smooth_dec(parts, 0, smooth.at[0])
    for s in range(3):
        if s < 2:
            smooth_dec(parts, s + 1, smooth.at[(s + 1) % 2])
        squares = boxcar_sums(smooth.at[s % 2], rows, result.at[pl.ds(2 * s, 2)])
        for b, width in enumerate(boxcar_widths):
            square = jnp.where(gone, 0.0, squares[b])
            across = square + jnp.where(no_side | gone, 0.0, beside[b][s])
            across = across + jnp.where(lane == 0, 0.0, pltpu.roll(square, 1, 1))
            across = across + jnp.where(lane == LANES - 1, 0.0, pltpu.roll(square, LANES - 1, 1))
            boxed = []
            at = 0
            for first, length, before, after in runs:
                at = at + 8
                framed[b, at : at + length] = across[first : first + length]
                framed[b, at - 1 : at] = across[before : before + 1]
                framed[b, at + length : at + length + 1] = across[after : after + 1]
                boxed.append(
                    framed[b, at - 1 : at - 1 + length]
                    + framed[b, at : at + length]
                    + framed[b, at + 1 : at + 1 + length]
                )
                at = at + length + 8
            boxed = jnp.concatenate(boxed, axis=0) if len(boxed) > 1 else boxed[0]
            scale = 1.0 / jnp.sqrt(boxed / (9.0 * channels) + width * width * epsilon)
            for c in range(channels):
                result[2 * s + b, c] = result[2 * s + b, c] * scale
            for k, (first, length, _, _) in enumerate(runs):
                copy = pltpu.make_async_copy(
                    result.at[2 * s + b, :, pl.ds(first, length), :],
                    targets(s, b)[k],
                    sems.at[len(runs) * (2 * s + b) + k],
                )
                copy.start()
                copies.append(copy)
    for copy in copies:
        copy.wait()


def inner_kernel(
    edge_ref, middle_ref, far_middle_ref, ra_ref, dec_ref, box_ref, gather_ref,
    out_ref, done_ref, edges_ref,
    source, smooth, result, framed, sems,
    *, batch,
):
    channels = 2 * edge_ref.shape[0]
    near = (lax.axis_index("ra") // 4) % 2
    edges_ref[...] = jnp.zeros_like(edges_ref)
    halves_of = ((edge_ref, HALF), (middle_ref, HALF)), ((edge_ref, 0), (far_middle_ref, 0))
    for part, parts in enumerate(halves_of):
        half_z = near if part == 0 else 1 - near
        for step in range(channels // 2 // batch):
            channels_at = []
            for j in range(batch):
                i = step * batch + j
                for half, (ref, at) in enumerate(parts):
                    packed = ref[i, at + 32 : at + HALF, :]
                    for k in range(2):
                        main = ref[i, at + 16 * k : at + 16 * k + 16, :]
                        put_rows(
                            source.at[part], j * ROWS + 32 * half + 16 * k, main,
                            (packed, packed), (64 * k, 64 * k + 32),
                        )
                channels_at.append(8 * (i // 4) + 4 * half_z + i % 4)
            smooth_ra(source.at[part], ra_ref, ROWS, channels_at, done_ref, edges_ref)
    beside = beside_squares([(dec_ref, edges_ref)], box_ref, gather_ref)

    def targets(s, b):
        return [out_ref.at[s, b, :, pl.ds(EDGE, ROWS - 2 * EDGE), :]]

    snr_rows(
        [(dec_ref, done_ref)], beside, (), inner_runs, targets, smooth, result, framed, sems
    )


def outer_kernel(
    held_ref, above_ref, below_ref, done_ref, edges_ref,
    ra_ref, dec_ref, dec_halo_ref, box_ref, gather_ref,
    out_ref,
    source, halo_done, halo_edges, smooth, result, framed, sems,
    *, batch,
):
    del held_ref
    channels = done_ref.shape[2] // LANES
    near = (lax.axis_index("ra") // 4) % 2
    dec_at, dec_n = lax.axis_index("dec"), lax.axis_size("dec")
    halo_edges[...] = jnp.zeros_like(halo_edges)
    for step in range(channels // batch):
        channels_at = []
        for j in range(batch):
            at = step * batch + j
            part, i = at // (channels // 2), at % (channels // 2)
            for k, ref in enumerate((above_ref, below_ref)):
                row = channels * EDGE + 8 * (at // 2)
                packed = ref[row : row + 8, :]
                lanes = 64 * (at % 2)
                put_rows(
                    source.at[step % 2], 2 * EDGE * j + EDGE * k, ref[at * EDGE : (at + 1) * EDGE, :],
                    (packed, packed), (lanes, lanes + 32),
                )
            half_z = near if part == 0 else 1 - near
            channels_at.append(8 * (i // 4) + 4 * half_z + i % 4)
        smooth_ra(source.at[step % 2], ra_ref, 2 * EDGE, channels_at, halo_done, halo_edges)
    parts = [(dec_ref, done_ref), (dec_halo_ref, halo_done)]
    beside = beside_squares(
        [(dec_ref, edges_ref), (dec_halo_ref, halo_edges)], box_ref, gather_ref
    )

    def targets(s, b):
        return [out_ref.at[s, b, :, pl.ds(at, EDGE), :] for at in (0, ROWS - EDGE)]

    outside = ((32, dec_at == 0), (35, dec_at == dec_n - 1))
    snr_rows(parts, beside, outside, outer_runs, targets, smooth, result, framed, sems)


def local(cube):
    tiles = channels = lax.axis_size("ra")
    vmem = pl.BlockSpec(memory_space=pltpu.VMEM)
    f32 = jnp.float32

    def call(kernel, shapes, operands, name, outside=(), scratch=()):
        return pl.pallas_call(
            kernel,
            out_shape=shapes,
            in_specs=[pl.BlockSpec(memory_space=pl.ANY)] * len(outside) + [vmem] * len(operands),
            out_specs=jax.tree.map(lambda _: vmem, shapes),
            scratch_shapes=scratch,
            compiler_params=pltpu.CompilerParams(vmem_limit_bytes=32 * 2**20),
            name=name,
        )(*outside, *operands)

    across = [(i, i ^ 4) for i in range(tiles)]
    groups = [[8 * x + 4 * z + y for x in range(tiles // 8) for y in range(4)] for z in range(2)]

    def regroup(chunks):
        return lax.all_to_all(
            chunks, "ra", split_axis=0, concat_axis=0, tiled=True, axis_index_groups=groups
        )

    part = jax.ShapeDtypeStruct((tiles // 2 + 1, 32, LANES), f32)
    chunk = jax.ShapeDtypeStruct((tiles // 2, CHUNK, LANES), f32)
    rows = [pltpu.VMEM((32, cube.shape[2]), f32), pltpu.SemaphoreType.DMA((2,))]
    columns = functools.partial(column_kernel, tiles)
    part, near_part = call(columns, (part, part), (), "columns", (cube,), rows)
    part = lax.ppermute(part, "ra", across)

    def regroup_middle(cube):
        chunks = call(functools.partial(middle_kernel, tiles), chunk, (), "middle", (cube,), rows)
        return regroup(chunks)

    def nothing(cube):
        return jnp.zeros(chunk.shape, f32)

    middle = lax.cond(lax.axis_index("ra") >= 0, regroup_middle, nothing, cube)
    far_middle = lax.ppermute(middle[:, :HALF], "ra", across)
    edge = call(edge_rows_kernel, chunk, (part, near_part), "edge_rows", (middle,))
    edge_chunk = regroup(edge)
    edge = jax.ShapeDtypeStruct((channels * (EDGE + 4), LANES), f32)
    top, bottom = call(edge_kernel, (edge, edge), (edge_chunk,), "edges")
    count = lax.axis_size("dec")
    down = [(i, i + 1) for i in range(count - 1)]
    up = [(i + 1, i) for i in range(count - 1)]
    above = lax.ppermute(bottom, "dec", down)
    below = lax.ppermute(top, "dec", up)
    box, gather = (jnp.asarray(value) for value in edge_weights(channels))
    along = jnp.asarray(ra_weights())
    anywhere = pl.BlockSpec(memory_space=pl.ANY)
    out = jax.ShapeDtypeStruct((3, 2, channels, ROWS, LANES), f32)
    batch = 8
    work = [
        pltpu.VMEM((2, OUT, channels * LANES), f32),
        pltpu.VMEM((6, channels, 2 * EDGE, LANES), f32),
        pltpu.VMEM((2, ROWS + 16, LANES), f32),
    ]
    params = pltpu.CompilerParams(vmem_limit_bytes=32 * 2**20)
    held, done, edges = pl.pallas_call(
        functools.partial(inner_kernel, batch=batch),
        out_shape=(
            out,
            jax.ShapeDtypeStruct((3, 2 * ROWS, channels * LANES), jnp.bfloat16),
            jax.ShapeDtypeStruct((2, ROWS, LANES), f32),
        ),
        in_specs=[vmem] * 7,
        out_specs=(anywhere, vmem, vmem),
        scratch_shapes=[pltpu.VMEM((2, batch * ROWS, 3 * LANES), jnp.bfloat16)]
        + work
        + [pltpu.SemaphoreType.DMA((6,))],
        compiler_params=params,
        cost_estimate=pl.CostEstimate(
            flops=2 * 10**9, bytes_accessed=8 * 2**20, transcendentals=0
        ),
        name="inner",
    )(
        edge_chunk, middle, far_middle, along,
        jnp.asarray(dec_weights(inner_out, tile_rows)), box, gather,
    )
    batch = 16
    return pl.pallas_call(
        functools.partial(outer_kernel, batch=batch),
        out_shape=out,
        in_specs=[anywhere] + [vmem] * 9,
        out_specs=anywhere,
        scratch_shapes=[
            pltpu.VMEM((2, batch * 2 * EDGE, 3 * LANES), jnp.bfloat16),
            pltpu.VMEM((3, 4 * EDGE, channels * LANES), jnp.bfloat16),
            pltpu.VMEM((2, 2 * EDGE, LANES), f32),
        ]
        + work
        + [pltpu.SemaphoreType.DMA((12,))],
        input_output_aliases={0: 0},
        compiler_params=params,
        cost_estimate=pl.CostEstimate(
            flops=10**9, bytes_accessed=8 * 2**20, transcendentals=0
        ),
        name="outer",
    )(
        held, above, below, done, edges, along,
        jnp.asarray(dec_weights(outer_out, tile_rows)),
        jnp.asarray(dec_weights(outer_out, halo_rows)), box, gather,
    )


def solution(mesh):
    return jax.shard_map(
        local,
        mesh=mesh,
        in_specs=(P("ra", "dec", None),),
        out_specs=P(None, None, None, "dec", "ra"),
        check_vma=False,
    )
```

```python
import functools

import jax
import jax.numpy as jnp
import ml_dtypes
import numpy as np
from jax import lax
from jax.experimental import pallas as pl
from jax.experimental.pallas import tpu as pltpu
from jax.sharding import PartitionSpec as P

sigma_values = (1, 2, 4)
boxcar_widths = (3, 7)
epsilon = 1e-06

LANES = 128
ROWS = 64
EDGE = 16
OUT = 40
STEP = 1024
HALF = 40
CHUNK = 2 * HALF
edge_rows = tuple(range(0, EDGE)) + tuple(range(ROWS - EDGE, ROWS))
middle_rows = tuple(range(EDGE, ROWS - EDGE))
tile_rows = edge_rows + middle_rows
above_rows, below_rows = tuple(range(-EDGE, 0)), tuple(range(ROWS, ROWS + EDGE))
inner_out = middle_rows + (EDGE - 1, ROWS - EDGE)
outer_out = edge_rows + (-1, EDGE, ROWS - EDGE - 1, ROWS)
inner_runs = ((0, 32, 32, 33),)
outer_runs = ((0, 16, 32, 33), (16, 16, 34, 35))
beside_cols = np.array(tuple(range(LANES, LANES + 16)) + tuple(range(-16, 0)))


def taps(distance, sigma):
    reach = 3 * sigma
    lags = np.arange(-reach, reach + 1, dtype=np.float64)
    weight_sum = np.sum(np.exp(-lags * lags / (2.0 * sigma * sigma)))
    value = np.exp(-(distance.astype(np.float64) ** 2) / (2.0 * sigma * sigma)) / weight_sum
    return np.where(np.abs(distance) <= reach, value, 0.0).astype(np.float32)


def halves(value):
    high = value.astype(ml_dtypes.bfloat16)
    low = (value - high.astype(np.float32)).astype(ml_dtypes.bfloat16)
    return high, low


def ra_weights():
    def band(cols):
        weights = np.zeros((len(cols), 4 * LANES), np.float32)
        for s, sigma in enumerate(sigma_values):
            weights[:, s * LANES : (s + 1) * LANES] = taps(
                cols[:, None] - np.arange(LANES)[None, :], sigma
            )
            for side, col in enumerate((-1, LANES)):
                weights[:, 3 * LANES + 32 * s + side] = taps(cols - col, sigma)
        return halves(weights)

    high, low = band(np.arange(LANES))
    beside_high, beside_low = band(beside_cols)
    nothing = np.zeros_like(beside_high)
    parts = [high, high, low, beside_high, beside_high, beside_low, nothing]
    return np.concatenate(parts, axis=0)


def dec_weights(out_rows, in_rows):
    result = np.zeros((3, 2 * OUT, 2 * len(in_rows)), ml_dtypes.bfloat16)
    for s, sigma in enumerate(sigma_values):
        weights = taps(np.array(in_rows)[None, :] - np.array(out_rows)[:, None], sigma)
        high, low = halves(weights)
        result[s, : len(out_rows), : len(in_rows)] = high
        result[s, : len(out_rows), len(in_rows) :] = high
        result[s, OUT : OUT + len(out_rows), : len(in_rows)] = low
    return result


def edge_weights(channels):
    half = channels // 2
    lane = np.arange(2 * LANES)
    tile, within = lane // LANES, lane % LANES
    sigma, slot = within // 32, within % 32
    channel, side = tile * half + slot // 2, slot % 2
    used = (sigma < 3) & (slot < 2 * half)
    same = used[:, None] & used[None, :] & (sigma[:, None] == sigma[None, :])
    same &= side[:, None] == side[None, :]
    boxcars = [
        same & (np.abs(channel[:, None] - channel[None, :]) <= width // 2)
        for width in boxcar_widths
    ]
    gathers = np.zeros((3, 2 * LANES, LANES), bool)
    for s in range(3):
        gathers[s, :, 0] = used & (sigma == s) & (side == 0)
        gathers[s, :, LANES - 1] = used & (sigma == s) & (side == 1)
    return (
        np.concatenate(boxcars, axis=1).astype(ml_dtypes.bfloat16),
        np.concatenate(gathers, axis=1).astype(ml_dtypes.bfloat16),
    )


def lane_index(shape):
    return lax.broadcasted_iota(jnp.int32, shape, len(shape) - 1)


def split(value):
    high = value.astype(jnp.bfloat16)
    low = (value - high.astype(jnp.float32)).astype(jnp.bfloat16)
    return high, low


def dot(a, b):
    return jnp.dot(a, b, preferred_element_type=jnp.float32)


def pack_rows(block, out_ref, tile, at):
    lane = lane_index((8, LANES))
    here, right, left = block
    packed = jnp.zeros((8, LANES), jnp.float32)
    for group in range(4):
        out_ref[tile, at + 8 * group : at + 8 * group + 8, :] = here(group)
        first, first_at = right(group)
        last, last_at = left(group)
        first = turn(first, 32 * group - first_at)
        last = turn(last, 32 * group + 16 - last_at)
        lanes = lane - 32 * group
        packed = jnp.where((lanes >= 0) & (lanes < 16), first, packed)
        packed = jnp.where((lanes >= 16) & (lanes < 32), last, packed)
    out_ref[tile, at + 32 : at + HALF, :] = packed


def turn(value, lanes):
    lanes = lanes % LANES
    return pltpu.roll(value, lanes, 1) if lanes else value


def far_half():
    return 1 - (lax.axis_index("ra") // 4) % 2


def rows_copies(cube_ref, rows, held, sems):
    copies = []
    for k, at in enumerate(range(0, len(rows), 16)):
        source = cube_ref.at[0, pl.ds(rows[at], 16), :]
        copies.append(pltpu.make_async_copy(source, held.at[pl.ds(at, 16), :], sems.at[k]))
    for copy in copies:
        copy.start()
    return copies


def column_kernel(tiles, cube_ref, far_ref, near_ref, held, sems):
    copies = rows_copies(cube_ref, edge_rows, held, sems)
    far = far_half()
    lane = lane_index((8, LANES))
    wide = tiles // 8

    def columns(tile, at):
        return held[at : at + 8, pl.ds(pl.multiple_of(tile * LANES, LANES), LANES)]

    for group in range(4):
        at = 8 * group
        if group % 2 == 0:
            copies[group // 2].wait()
        for half_z, out_ref in ((far, far_ref), (1 - far, near_ref)):
            beside = jnp.zeros((8, LANES), jnp.float32)
            for x in range(wide):
                first = 8 * x + 4 * half_z
                for y in range(4):
                    out_ref[4 * x + y, at : at + 8, :] = columns(first + y, at)
                right = turn(columns(jnp.minimum(first + 4, tiles - 1), at), 32 * x)
                left = turn(columns(jnp.maximum(first - 1, 0), at), 32 * x + 32)
                right = jnp.where(first + 4 < tiles, right, 0.0)
                left = jnp.where(first > 0, left, 0.0)
                lanes = lane - 32 * x
                beside = jnp.where((lanes >= 0) & (lanes < 16), right, beside)
                beside = jnp.where((lanes >= 16) & (lanes < 32), left, beside)
            out_ref[4 * wide, at : at + 8, :] = beside


def pack_cube(tiles, held, half_z, out_ref, at):
    def columns(tile, group):
        inside = (tile >= 0) & (tile < tiles)
        tile = jnp.clip(tile, 0, tiles - 1)
        lanes = pl.ds(pl.multiple_of(tile * LANES, LANES), LANES)
        return inside, held[8 * group : 8 * group + 8, lanes]

    for x in range(tiles // 8):
        for y in range(4):
            tile = 8 * x + 4 * half_z + y

            def here(group):
                return columns(tile, group)[1]

            def right(group):
                inside, value = columns(tile + 1, group)
                return (jnp.where(inside, value, 0.0) if y == 3 else value), 0

            def left(group):
                inside, value = columns(tile - 1, group)
                return (jnp.where(inside, value, 0.0) if y == 0 else value), LANES - 16

            pack_rows((here, right, left), out_ref, 4 * x + y, at)


def middle_kernel(tiles, cube_ref, out_ref, held, sems):
    for copy in rows_copies(cube_ref, middle_rows, held, sems):
        copy.wait()
    far = far_half()
    pack_cube(tiles, held, far, out_ref, 0)
    pack_cube(tiles, held, 1 - far, out_ref, HALF)


def edge_rows_kernel(after_ref, far_ref, near_ref, out_ref):
    del after_ref
    wide = out_ref.shape[0] // 4
    for start, ref in ((0, far_ref), (HALF, near_ref)):
        for x in range(wide):
            for y in range(4):
                tile = 4 * x + y

                def here(group):
                    return ref[tile, 8 * group : 8 * group + 8, :]

                def right(group):
                    if y < 3:
                        return ref[tile + 1, 8 * group : 8 * group + 8, :], 0
                    return ref[4 * wide, 8 * group : 8 * group + 8, :], 32 * x

                def left(group):
                    if y > 0:
                        return ref[tile - 1, 8 * group : 8 * group + 8, :], LANES - 16
                    return ref[4 * wide, 8 * group : 8 * group + 8, :], 32 * x + 16

                pack_rows((here, right, left), out_ref, tile, start)


def edge_kernel(edge_ref, chip_ref, next_ref):
    odd = lax.axis_index("dec") % 2
    count = edge_ref.shape[0]
    channels = 2 * count
    lane = lane_index((8, LANES))
    for ref, lower in ((chip_ref, 1 - odd), (next_ref, odd)):
        rows = pl.multiple_of(EDGE * lower, EDGE)
        for part, start in enumerate((HALF, 0)):
            for i in range(count):
                at = (part * count + i) * EDGE
                ref[at : at + EDGE, :] = edge_ref[i, pl.ds(start + rows, EDGE), :]
            for pair in range(count // 2):
                at = channels * EDGE + 8 * (part * count // 2 + pair)
                first = edge_ref[2 * pair, start + 32 : start + HALF, :]
                second = edge_ref[2 * pair + 1, start + 32 : start + HALF, :]
                upper_halves = jnp.where(lane < 64, first, pltpu.roll(second, 64, 1))
                lower_halves = jnp.where(lane < 64, pltpu.roll(first, 64, 1), second)
                ref[at : at + 8, :] = jnp.where(lower == 1, lower_halves, upper_halves)


def put_rows(source, at, main, packed, places):
    lane = lane_index((8, LANES))
    high, low = split(main)
    beside = []
    for value, place in zip(packed, places):
        value_high = value.astype(jnp.bfloat16).astype(jnp.float32)
        value_low = value - value_high
        mix = jnp.where(lane < 64, turn(value_low, 32 - place), turn(value_high, 64 - place))
        mix = jnp.where(lane < 32, turn(value_high, -place), mix)
        beside.append(jnp.where(lane < 96, mix, 0.0))
    source[at : at + 16, :LANES] = low
    source[at : at + 16, LANES : 2 * LANES] = high
    source[at : at + 16, 2 * LANES :] = jnp.concatenate(beside, axis=0).astype(jnp.bfloat16)


def smooth_ra(source, weights_ref, rows, channels_at, done, edges):
    operand = jnp.concatenate([source[:, : 2 * LANES], source[:, LANES:]], axis=1)
    along = dot(operand, weights_ref[...])
    half = done.shape[2] // LANES // 2
    for j, c in enumerate(channels_at):
        block = along[j * rows : (j + 1) * rows]
        lanes = pl.ds(pl.multiple_of(c * LANES, LANES), LANES)
        for s in range(3):
            high, low = split(block[:, s * LANES : (s + 1) * LANES])
            done[s, :rows, lanes] = high
            done[s, rows:, lanes] = low
        tile, slot = c // half, c % half
        edges[tile] = edges[tile] + pltpu.roll(block[:, 3 * LANES :], 2 * slot, 1)


def smooth_dec(parts, s, out):
    for at in range(0, out.shape[1], STEP):
        both = sum(dot(weights[s], done[s, :, at : at + STEP]) for weights, done in parts)
        out[:, at : at + STEP] = both[:OUT] + both[OUT:]


def beside_squares(parts, box_ref, gather_ref):
    which = lane_index((OUT, 2 * LANES)) % LANES // 32
    smoothed = jnp.zeros((OUT, 2 * LANES), jnp.float32)
    parts = [
        (weights, jnp.concatenate(split(jnp.concatenate([edges[0], edges[1]], axis=1)), axis=0))
        for weights, edges in parts
    ]
    for s in range(3):
        both = sum(dot(weights[s], value) for weights, value in parts)
        smoothed = jnp.where(which == s, both[:OUT] + both[OUT:], smoothed)
    high, low = split(smoothed)
    summed = dot(high, box_ref[...]) + dot(low, box_ref[...])
    summed = jnp.concatenate([summed[:, : 2 * LANES], summed[:, 2 * LANES :]], axis=0)
    high, low = split(summed * summed)
    squares = dot(high, gather_ref[...]) + dot(low, gather_ref[...])
    return [
        [squares[b * OUT : (b + 1) * OUT, s * LANES : (s + 1) * LANES] for s in range(3)]
        for b in range(2)
    ]


def boxcar_sums(smooth, rows, result):
    channels = result.shape[1]
    squares = [[], []]
    for at in range(0, OUT, 8):
        planes = {
            c: smooth[at : at + 8, c * LANES : (c + 1) * LANES] for c in range(channels)
        }

        def total(places):
            return functools.reduce(jnp.add, [planes[c] for c in places if c in planes])

        triples = {c: total(range(c - 1, c + 2)) for c in range(-1, channels + 1)}
        totals = [[None, None], [None, None]]
        for c in range(channels):
            terms = [triples[c - 2]] if c >= 1 else []
            terms += [triples[c + 1]] + ([planes[c + 3]] if c + 3 < channels else [])
            for b, value in enumerate((triples[c], functools.reduce(jnp.add, terms))):
                if at < rows:
                    result[b, c, at : at + 8, :] = value
                square = value * value
                before = totals[b][c % 2]
                totals[b][c % 2] = square if before is None else before + square
        for b in range(2):
            squares[b].append(totals[b][0] + totals[b][1])
    return [jnp.concatenate(square, axis=0) for square in squares]


def snr_rows(parts, beside, outside, runs, targets, smooth, result, framed, sems):
    channels = result.shape[1]
    ra_at, ra_n = lax.axis_index("ra"), lax.axis_size("ra")
    lane = lane_index((OUT, LANES))
    row = lax.broadcasted_iota(jnp.int32, (OUT, LANES), 0)
    gone = row < 0
    for at, condition in outside:
        gone = gone | ((row == at) & condition)
    no_side = ((lane == 0) & (ra_at == 0)) | ((lane == LANES - 1) & (ra_at == ra_n - 1))
    rows = sum(run[1] for run in runs)
    copies = []
    smooth_dec(parts, 0, smooth.at[0])
    for s in range(3):
        if s < 2:
            smooth_dec(parts, s + 1, smooth.at[(s + 1) % 2])
        squares = boxcar_sums(smooth.at[s % 2], rows, result.at[pl.ds(2 * s, 2)])
        for b, width in enumerate(boxcar_widths):
            square = jnp.where(gone, 0.0, squares[b])
            across = square + jnp.where(no_side | gone, 0.0, beside[b][s])
            across = across + jnp.where(lane == 0, 0.0, pltpu.roll(square, 1, 1))
            across = across + jnp.where(lane == LANES - 1, 0.0, pltpu.roll(square, LANES - 1, 1))
            boxed = []
            at = 0
            for first, length, before, after in runs:
                at = at + 8
                framed[b, at : at + length] = across[first : first + length]
                framed[b, at - 1 : at] = across[before : before + 1]
                framed[b, at + length : at + length + 1] = across[after : after + 1]
                boxed.append(
                    framed[b, at - 1 : at - 1 + length]
                    + framed[b, at : at + length]
                    + framed[b, at + 1 : at + 1 + length]
                )
                at = at + length + 8
            boxed = jnp.concatenate(boxed, axis=0) if len(boxed) > 1 else boxed[0]
            scale = 1.0 / jnp.sqrt(boxed / (9.0 * channels) + width * width * epsilon)
            for c in range(channels):
                result[2 * s + b, c] = result[2 * s + b, c] * scale
            for k, (first, length, _, _) in enumerate(runs):
                copy = pltpu.make_async_copy(
                    result.at[2 * s + b, :, pl.ds(first, length), :],
                    targets(s, b)[k],
                    sems.at[len(runs) * (2 * s + b) + k],
                )
                copy.start()
                copies.append(copy)
    for copy in copies:
        copy.wait()


def inner_kernel(
    edge_ref, middle_ref, far_middle_ref, ra_ref, dec_ref, box_ref, gather_ref,
    out_ref, done_ref, edges_ref,
    source, smooth, result, framed, sems,
    *, batch,
):
    channels = 2 * edge_ref.shape[0]
    near = (lax.axis_index("ra") // 4) % 2
    edges_ref[...] = jnp.zeros_like(edges_ref)
    halves_of = ((edge_ref, HALF), (middle_ref, HALF)), ((edge_ref, 0), (far_middle_ref, 0))
    for part, parts in enumerate(halves_of):
        half_z = near if part == 0 else 1 - near
        for step in range(channels // 2 // batch):
            channels_at = []
            for j in range(batch):
                i = step * batch + j
                for half, (ref, at) in enumerate(parts):
                    packed = ref[i, at + 32 : at + HALF, :]
                    for k in range(2):
                        main = ref[i, at + 16 * k : at + 16 * k + 16, :]
                        put_rows(
                            source.at[part], j * ROWS + 32 * half + 16 * k, main,
                            (packed, packed), (64 * k, 64 * k + 32),
                        )
                channels_at.append(8 * (i // 4) + 4 * half_z + i % 4)
            smooth_ra(source.at[part], ra_ref, ROWS, channels_at, done_ref, edges_ref)
    beside = beside_squares([(dec_ref, edges_ref)], box_ref, gather_ref)

    def targets(s, b):
        return [out_ref.at[s, b, :, pl.ds(EDGE, ROWS - 2 * EDGE), :]]

    snr_rows(
        [(dec_ref, done_ref)], beside, (), inner_runs, targets, smooth, result, framed, sems
    )


def outer_kernel(
    held_ref, chip_ref, next_ref, done_ref, edges_ref,
    ra_ref, dec_ref, dec_halo_ref, box_ref, gather_ref,
    out_ref,
    source, halo_done, halo_edges, smooth, result, framed, sems,
    *, batch,
):
    del held_ref
    channels = done_ref.shape[2] // LANES
    near = (lax.axis_index("ra") // 4) % 2
    dec_at, dec_n = lax.axis_index("dec"), lax.axis_size("dec")
    halo_edges[...] = jnp.zeros_like(halo_edges)
    for step in range(channels // batch):
        channels_at = []
        for j in range(batch):
            at = step * batch + j
            part, i = at // (channels // 2), at % (channels // 2)
            for k, ref in enumerate((chip_ref, next_ref)):
                row = channels * EDGE + 8 * (at // 2)
                packed = ref[row : row + 8, :]
                lanes = 64 * (at % 2)
                put_rows(
                    source.at[step % 2], 2 * EDGE * j + EDGE * k, ref[at * EDGE : (at + 1) * EDGE, :],
                    (packed, packed), (lanes, lanes + 32),
                )
            half_z = near if part == 0 else 1 - near
            channels_at.append(8 * (i // 4) + 4 * half_z + i % 4)
        smooth_ra(source.at[step % 2], ra_ref, 2 * EDGE, channels_at, halo_done, halo_edges)
    dec_halo_ref = dec_halo_ref.at[dec_at % 2]
    parts = [(dec_ref, done_ref), (dec_halo_ref, halo_done)]
    beside = beside_squares(
        [(dec_ref, edges_ref), (dec_halo_ref, halo_edges)], box_ref, gather_ref
    )

    def targets(s, b):
        return [out_ref.at[s, b, :, pl.ds(at, EDGE), :] for at in (0, ROWS - EDGE)]

    outside = ((32, dec_at == 0), (35, dec_at == dec_n - 1))
    snr_rows(parts, beside, outside, outer_runs, targets, smooth, result, framed, sems)


def local(cube):
    tiles = channels = lax.axis_size("ra")
    vmem = pl.BlockSpec(memory_space=pltpu.VMEM)
    f32 = jnp.float32

    def call(kernel, shapes, operands, name, outside=(), scratch=()):
        return pl.pallas_call(
            kernel,
            out_shape=shapes,
            in_specs=[pl.BlockSpec(memory_space=pl.ANY)] * len(outside) + [vmem] * len(operands),
            out_specs=jax.tree.map(lambda _: vmem, shapes),
            scratch_shapes=scratch,
            compiler_params=pltpu.CompilerParams(vmem_limit_bytes=32 * 2**20),
            name=name,
        )(*outside, *operands)

    across = [(i, i ^ 4) for i in range(tiles)]
    groups = [[8 * x + 4 * z + y for x in range(tiles // 8) for y in range(4)] for z in range(2)]

    def regroup(chunks):
        return lax.all_to_all(
            chunks, "ra", split_axis=0, concat_axis=0, tiled=True, axis_index_groups=groups
        )

    part = jax.ShapeDtypeStruct((tiles // 2 + 1, 32, LANES), f32)
    chunk = jax.ShapeDtypeStruct((tiles // 2, CHUNK, LANES), f32)
    rows = [pltpu.VMEM((32, cube.shape[2]), f32), pltpu.SemaphoreType.DMA((2,))]
    columns = functools.partial(column_kernel, tiles)
    part, near_part = call(columns, (part, part), (), "columns", (cube,), rows)
    part = lax.ppermute(part, "ra", across)

    def regroup_middle(cube):
        chunks = call(functools.partial(middle_kernel, tiles), chunk, (), "middle", (cube,), rows)
        return regroup(chunks)

    def nothing(cube):
        return jnp.zeros(chunk.shape, f32)

    middle = lax.cond(lax.axis_index("ra") >= 0, regroup_middle, nothing, cube)
    far_middle = lax.ppermute(middle[:, :HALF], "ra", across)

    def regroup_edges(part, near_part, middle):
        chunks = call(edge_rows_kernel, chunk, (part, near_part), "edge_rows", (middle,))
        chunks = regroup(chunks)
        return (chunks, *call(edge_kernel, (edge, edge), (chunks,), "edges"))

    def no_edges(part, near_part, middle):
        return jnp.zeros(chunk.shape, f32), jnp.zeros(edge.shape, f32), jnp.zeros(edge.shape, f32)

    edge = jax.ShapeDtypeStruct((channels * (EDGE + 4), LANES), f32)
    edge_chunk, for_chip, for_next = lax.cond(
        lax.axis_index("ra") >= 0, regroup_edges, no_edges, part, near_part, middle
    )
    count = lax.axis_size("dec")
    on_chip = [(i, i ^ 1) for i in range(count)]
    beyond = [(i, i + 1) for i in range(1, count - 1, 2)] + [(i + 1, i) for i in range(1, count - 1, 2)]
    from_chip = lax.ppermute(for_chip, "dec", on_chip)
    from_next = lax.ppermute(for_next, "dec", beyond)
    box, gather = (jnp.asarray(value) for value in edge_weights(channels))
    along = jnp.asarray(ra_weights())
    anywhere = pl.BlockSpec(memory_space=pl.ANY)
    out = jax.ShapeDtypeStruct((3, 2, channels, ROWS, LANES), f32)
    batch = 8
    work = [
        pltpu.VMEM((2, OUT, channels * LANES), f32),
        pltpu.VMEM((6, channels, 2 * EDGE, LANES), f32),
        pltpu.VMEM((2, ROWS + 16, LANES), f32),
    ]
    params = pltpu.CompilerParams(vmem_limit_bytes=32 * 2**20)
    held, done, edges = pl.pallas_call(
        functools.partial(inner_kernel, batch=batch),
        out_shape=(
            out,
            jax.ShapeDtypeStruct((3, 2 * ROWS, channels * LANES), jnp.bfloat16),
            jax.ShapeDtypeStruct((2, ROWS, LANES), f32),
        ),
        in_specs=[vmem] * 7,
        out_specs=(anywhere, vmem, vmem),
        scratch_shapes=[pltpu.VMEM((2, batch * ROWS, 3 * LANES), jnp.bfloat16)]
        + work
        + [pltpu.SemaphoreType.DMA((6,))],
        compiler_params=params,
        cost_estimate=pl.CostEstimate(
            flops=2 * 10**9, bytes_accessed=8 * 2**20, transcendentals=0
        ),
        name="inner",
    )(
        edge_chunk, middle, far_middle, along,
        jnp.asarray(dec_weights(inner_out, tile_rows)), box, gather,
    )
    batch = 16
    halo_weights = np.stack(
        [dec_weights(outer_out, rows) for rows in (below_rows + above_rows, above_rows + below_rows)]
    )
    return pl.pallas_call(
        functools.partial(outer_kernel, batch=batch),
        out_shape=out,
        in_specs=[anywhere] + [vmem] * 9,
        out_specs=anywhere,
        scratch_shapes=[
            pltpu.VMEM((2, batch * 2 * EDGE, 3 * LANES), jnp.bfloat16),
            pltpu.VMEM((3, 4 * EDGE, channels * LANES), jnp.bfloat16),
            pltpu.VMEM((2, 2 * EDGE, LANES), f32),
        ]
        + work
        + [pltpu.SemaphoreType.DMA((12,))],
        input_output_aliases={0: 0},
        compiler_params=params,
        cost_estimate=pl.CostEstimate(
            flops=10**9, bytes_accessed=8 * 2**20, transcendentals=0
        ),
        name="outer",
    )(
        held, from_chip, from_next, done, edges, along,
        jnp.asarray(dec_weights(outer_out, tile_rows)),
        jnp.asarray(halo_weights), box, gather,
    )


def solution(mesh):
    return jax.shard_map(
        local,
        mesh=mesh,
        in_specs=(P("ra", "dec", None),),
        out_specs=P(None, None, None, "dec", "ra"),
        check_vma=False,
    )
```

```python
import functools

import jax
import jax.numpy as jnp
import ml_dtypes
import numpy as np
from jax import lax
from jax.experimental import pallas as pl
from jax.experimental.pallas import tpu as pltpu
from jax.sharding import PartitionSpec as P

sigma_values = (1, 2, 4)
boxcar_widths = (3, 7)
epsilon = 1e-06

LANES = 128
ROWS = 64
EDGE = 16
OUT = 40
STEP = 1024
HALF = 40
CHUNK = 2 * HALF
edge_rows = tuple(range(0, EDGE)) + tuple(range(ROWS - EDGE, ROWS))
middle_rows = tuple(range(EDGE, ROWS - EDGE))
tile_rows = edge_rows + middle_rows
above_rows, below_rows = tuple(range(-EDGE, 0)), tuple(range(ROWS, ROWS + EDGE))
inner_out = middle_rows + (EDGE - 1, ROWS - EDGE)
outer_out = edge_rows + (-1, EDGE, ROWS - EDGE - 1, ROWS)
inner_runs = ((0, 32, 32, 33),)
outer_runs = ((0, 16, 32, 33), (16, 16, 34, 35))
beside_cols = np.array(tuple(range(LANES, LANES + 16)) + tuple(range(-16, 0)))


def taps(distance, sigma):
    reach = 3 * sigma
    lags = np.arange(-reach, reach + 1, dtype=np.float64)
    weight_sum = np.sum(np.exp(-lags * lags / (2.0 * sigma * sigma)))
    value = np.exp(-(distance.astype(np.float64) ** 2) / (2.0 * sigma * sigma)) / weight_sum
    return np.where(np.abs(distance) <= reach, value, 0.0).astype(np.float32)


def halves(value):
    high = value.astype(ml_dtypes.bfloat16)
    low = (value - high.astype(np.float32)).astype(ml_dtypes.bfloat16)
    return high, low


def ra_weights():
    def band(cols):
        weights = np.zeros((len(cols), 4 * LANES), np.float32)
        for s, sigma in enumerate(sigma_values):
            weights[:, s * LANES : (s + 1) * LANES] = taps(
                cols[:, None] - np.arange(LANES)[None, :], sigma
            )
            for side, col in enumerate((-1, LANES)):
                weights[:, 3 * LANES + 32 * s + side] = taps(cols - col, sigma)
        return halves(weights)

    high, low = band(np.arange(LANES))
    beside_high, beside_low = band(beside_cols)
    nothing = np.zeros_like(beside_high)
    parts = [high, high, low, beside_high, beside_high, beside_low, nothing]
    return np.concatenate(parts, axis=0)


def dec_weights(out_rows, in_rows):
    result = np.zeros((3, 2 * OUT, 2 * len(in_rows)), ml_dtypes.bfloat16)
    for s, sigma in enumerate(sigma_values):
        weights = taps(np.array(in_rows)[None, :] - np.array(out_rows)[:, None], sigma)
        high, low = halves(weights)
        result[s, : len(out_rows), : len(in_rows)] = high
        result[s, : len(out_rows), len(in_rows) :] = high
        result[s, OUT : OUT + len(out_rows), : len(in_rows)] = low
    return result


def edge_weights(channels):
    half = channels // 2
    lane = np.arange(2 * LANES)
    tile, within = lane // LANES, lane % LANES
    sigma, slot = within // 32, within % 32
    channel, side = tile * half + slot // 2, slot % 2
    used = (sigma < 3) & (slot < 2 * half)
    same = used[:, None] & used[None, :] & (sigma[:, None] == sigma[None, :])
    same &= side[:, None] == side[None, :]
    boxcars = [
        same & (np.abs(channel[:, None] - channel[None, :]) <= width // 2)
        for width in boxcar_widths
    ]
    gathers = np.zeros((3, 2 * LANES, LANES), bool)
    for s in range(3):
        gathers[s, :, 0] = used & (sigma == s) & (side == 0)
        gathers[s, :, LANES - 1] = used & (sigma == s) & (side == 1)
    return (
        np.concatenate(boxcars, axis=1).astype(ml_dtypes.bfloat16),
        np.concatenate(gathers, axis=1).astype(ml_dtypes.bfloat16),
    )


def lane_index(shape):
    return lax.broadcasted_iota(jnp.int32, shape, len(shape) - 1)


def split(value):
    high = value.astype(jnp.bfloat16)
    low = (value - high.astype(jnp.float32)).astype(jnp.bfloat16)
    return high, low


def dot(a, b):
    return jnp.dot(a, b, preferred_element_type=jnp.float32)


def pack_rows(block, out_ref, tile, at):
    lane = lane_index((8, LANES))
    here, right, left = block
    packed = jnp.zeros((8, LANES), jnp.float32)
    for group in range(4):
        out_ref[tile, at + 8 * group : at + 8 * group + 8, :] = here(group)
        first, first_at = right(group)
        last, last_at = left(group)
        first = turn(first, 32 * group - first_at)
        last = turn(last, 32 * group + 16 - last_at)
        lanes = lane - 32 * group
        packed = jnp.where((lanes >= 0) & (lanes < 16), first, packed)
        packed = jnp.where((lanes >= 16) & (lanes < 32), last, packed)
    out_ref[tile, at + 32 : at + HALF, :] = packed


def turn(value, lanes):
    lanes = lanes % LANES
    return pltpu.roll(value, lanes, 1) if lanes else value


def far_half():
    return 1 - (lax.axis_index("ra") // 4) % 2


def rows_copies(cube_ref, rows, held, sems):
    copies = []
    for k, at in enumerate(range(0, len(rows), 16)):
        source = cube_ref.at[0, pl.ds(rows[at], 16), :]
        copies.append(pltpu.make_async_copy(source, held.at[pl.ds(at, 16), :], sems.at[k]))
    for copy in copies:
        copy.start()
    return copies


def column_kernel(tiles, cube_ref, far_ref, near_ref, held, sems):
    copies = rows_copies(cube_ref, edge_rows, held, sems)
    far = far_half()
    lane = lane_index((8, LANES))
    wide = tiles // 8

    def columns(tile, at):
        return held[at : at + 8, pl.ds(pl.multiple_of(tile * LANES, LANES), LANES)]

    for group in range(4):
        at = 8 * group
        if group % 2 == 0:
            copies[group // 2].wait()
        for half_z, out_ref in ((far, far_ref), (1 - far, near_ref)):
            beside = jnp.zeros((8, LANES), jnp.float32)
            for x in range(wide):
                first = 8 * x + 4 * half_z
                for y in range(4):
                    out_ref[4 * x + y, at : at + 8, :] = columns(first + y, at)
                right = turn(columns(jnp.minimum(first + 4, tiles - 1), at), 32 * x)
                left = turn(columns(jnp.maximum(first - 1, 0), at), 32 * x + 32)
                right = jnp.where(first + 4 < tiles, right, 0.0)
                left = jnp.where(first > 0, left, 0.0)
                lanes = lane - 32 * x
                beside = jnp.where((lanes >= 0) & (lanes < 16), right, beside)
                beside = jnp.where((lanes >= 16) & (lanes < 32), left, beside)
            out_ref[4 * wide, at : at + 8, :] = beside


def pack_cube(tiles, held, half_z, out_ref, at):
    def columns(tile, group):
        inside = (tile >= 0) & (tile < tiles)
        tile = jnp.clip(tile, 0, tiles - 1)
        lanes = pl.ds(pl.multiple_of(tile * LANES, LANES), LANES)
        return inside, held[8 * group : 8 * group + 8, lanes]

    for x in range(tiles // 8):
        for y in range(4):
            tile = 8 * x + 4 * half_z + y

            def here(group):
                return columns(tile, group)[1]

            def right(group):
                inside, value = columns(tile + 1, group)
                return (jnp.where(inside, value, 0.0) if y == 3 else value), 0

            def left(group):
                inside, value = columns(tile - 1, group)
                return (jnp.where(inside, value, 0.0) if y == 0 else value), LANES - 16

            pack_rows((here, right, left), out_ref, 4 * x + y, at)


def middle_kernel(tiles, cube_ref, out_ref, held, sems):
    for copy in rows_copies(cube_ref, middle_rows, held, sems):
        copy.wait()
    far = far_half()
    pack_cube(tiles, held, far, out_ref, 0)
    pack_cube(tiles, held, 1 - far, out_ref, HALF)


def edge_rows_kernel(after_ref, far_ref, near_ref, out_ref):
    del after_ref
    wide = out_ref.shape[0] // 4
    for start, ref in ((0, far_ref), (HALF, near_ref)):
        for x in range(wide):
            for y in range(4):
                tile = 4 * x + y

                def here(group):
                    return ref[tile, 8 * group : 8 * group + 8, :]

                def right(group):
                    if y < 3:
                        return ref[tile + 1, 8 * group : 8 * group + 8, :], 0
                    return ref[4 * wide, 8 * group : 8 * group + 8, :], 32 * x

                def left(group):
                    if y > 0:
                        return ref[tile - 1, 8 * group : 8 * group + 8, :], LANES - 16
                    return ref[4 * wide, 8 * group : 8 * group + 8, :], 32 * x + 16

                pack_rows((here, right, left), out_ref, tile, start)


def edge_kernel(outside_ref, chip_ref, next_ref, edge_ref, sem):
    fetch = pltpu.make_async_copy(outside_ref, edge_ref, sem)
    fetch.start()
    fetch.wait()
    odd = lax.axis_index("dec") % 2
    count = edge_ref.shape[0]
    channels = 2 * count
    lane = lane_index((8, LANES))
    for ref, lower in ((chip_ref, 1 - odd), (next_ref, odd)):
        rows = pl.multiple_of(EDGE * lower, EDGE)
        for part, start in enumerate((HALF, 0)):
            for i in range(count):
                at = (part * count + i) * EDGE
                ref[at : at + EDGE, :] = edge_ref[i, pl.ds(start + rows, EDGE), :]
            for pair in range(count // 2):
                at = channels * EDGE + 8 * (part * count // 2 + pair)
                first = edge_ref[2 * pair, start + 32 : start + HALF, :]
                second = edge_ref[2 * pair + 1, start + 32 : start + HALF, :]
                upper_halves = jnp.where(lane < 64, first, pltpu.roll(second, 64, 1))
                lower_halves = jnp.where(lane < 64, pltpu.roll(first, 64, 1), second)
                ref[at : at + 8, :] = jnp.where(lower == 1, lower_halves, upper_halves)


def put_rows(source, at, main, packed, places):
    lane = lane_index((8, LANES))
    high, low = split(main)
    beside = []
    for value, place in zip(packed, places):
        value_high = value.astype(jnp.bfloat16).astype(jnp.float32)
        value_low = value - value_high
        mix = jnp.where(lane < 64, turn(value_low, 32 - place), turn(value_high, 64 - place))
        mix = jnp.where(lane < 32, turn(value_high, -place), mix)
        beside.append(jnp.where(lane < 96, mix, 0.0))
    source[at : at + 16, :LANES] = low
    source[at : at + 16, LANES : 2 * LANES] = high
    source[at : at + 16, 2 * LANES :] = jnp.concatenate(beside, axis=0).astype(jnp.bfloat16)


def smooth_ra(source, weights_ref, rows, channels_at, done, edges):
    operand = jnp.concatenate([source[:, : 2 * LANES], source[:, LANES:]], axis=1)
    along = dot(operand, weights_ref[...])
    beside = {}
    for j, (i, half_z) in enumerate(channels_at):
        c = 8 * (i // 4) + 4 * half_z + i % 4
        block = along[j * rows : (j + 1) * rows]
        lanes = pl.ds(pl.multiple_of(c * LANES, LANES), LANES)
        for s in range(3):
            high, low = split(block[:, s * LANES : (s + 1) * LANES])
            done[s, :rows, lanes] = high
            done[s, rows:, lanes] = low
        value = turn(block[:, 3 * LANES :], 16 * (i // 4 % 2) + 2 * (i % 4))
        beside[i // 8] = beside[i // 8] + value if i // 8 in beside else value
    for tile, value in beside.items():
        edges[tile] = edges[tile] + pltpu.roll(value, 8 * half_z, 1)


def smooth_dec(parts, s, out):
    for at in range(0, out.shape[1], STEP):
        both = sum(dot(weights[s], done[s, :, at : at + STEP]) for weights, done in parts)
        out[:, at : at + STEP] = both[:OUT] + both[OUT:]


def beside_squares(parts, box_ref, gather_ref):
    which = lane_index((OUT, 2 * LANES)) % LANES // 32
    smoothed = jnp.zeros((OUT, 2 * LANES), jnp.float32)
    parts = [
        (weights, jnp.concatenate(split(jnp.concatenate([edges[0], edges[1]], axis=1)), axis=0))
        for weights, edges in parts
    ]
    for s in range(3):
        both = sum(dot(weights[s], value) for weights, value in parts)
        smoothed = jnp.where(which == s, both[:OUT] + both[OUT:], smoothed)
    high, low = split(smoothed)
    summed = dot(high, box_ref[...]) + dot(low, box_ref[...])
    summed = jnp.concatenate([summed[:, : 2 * LANES], summed[:, 2 * LANES :]], axis=0)
    high, low = split(summed * summed)
    squares = dot(high, gather_ref[...]) + dot(low, gather_ref[...])
    return [
        [squares[b * OUT : (b + 1) * OUT, s * LANES : (s + 1) * LANES] for s in range(3)]
        for b in range(2)
    ]


def boxcar_sums(smooth, rows, result):
    channels = result.shape[1]
    squares = [[], []]
    for at in range(0, OUT, 8):
        planes = {
            c: smooth[at : at + 8, c * LANES : (c + 1) * LANES] for c in range(channels)
        }

        def total(places):
            return functools.reduce(jnp.add, [planes[c] for c in places if c in planes])

        triples = {c: total(range(c - 1, c + 2)) for c in range(-1, channels + 1)}
        totals = [[None, None], [None, None]]
        for c in range(channels):
            terms = [triples[c - 2]] if c >= 1 else []
            terms += [triples[c + 1]] + ([planes[c + 3]] if c + 3 < channels else [])
            for b, value in enumerate((triples[c], functools.reduce(jnp.add, terms))):
                if at < rows:
                    result[b, c, at : at + 8, :] = value
                square = value * value
                before = totals[b][c % 2]
                totals[b][c % 2] = square if before is None else before + square
        for b in range(2):
            squares[b].append(totals[b][0] + totals[b][1])
    return [jnp.concatenate(square, axis=0) for square in squares]


def snr_rows(parts, beside, outside, runs, smooth, result, framed, finished, last=None):
    channels = result.shape[1]
    ra_at, ra_n = lax.axis_index("ra"), lax.axis_size("ra")
    lane = lane_index((OUT, LANES))
    row = lax.broadcasted_iota(jnp.int32, (OUT, LANES), 0)
    gone = row < 0
    for at, condition in outside:
        gone = gone | ((row == at) & condition)
    no_side = ((lane == 0) & (ra_at == 0)) | ((lane == LANES - 1) & (ra_at == ra_n - 1))
    rows = sum(run[1] for run in runs)
    smooth_dec(parts, 0, smooth.at[0])
    for s in range(3):
        if s == 1:
            smooth_dec(parts, 2, smooth.at[0])
        squares = boxcar_sums(smooth.at[s % 2], rows, result.at[pl.ds(2 * s, 2)])
        if s == 0:
            beside = beside()
            smooth_dec(parts, 1, smooth.at[1])
        for b, width in enumerate(boxcar_widths):
            square = jnp.where(gone, 0.0, squares[b])
            across = square + jnp.where(no_side | gone, 0.0, beside[b][s])
            across = across + jnp.where(lane == 0, 0.0, pltpu.roll(square, 1, 1))
            across = across + jnp.where(lane == LANES - 1, 0.0, pltpu.roll(square, LANES - 1, 1))
            boxed = []
            at = 0
            for first, length, before, after in runs:
                at = at + 8
                framed[b, at : at + length] = across[first : first + length]
                framed[b, at - 1 : at] = across[before : before + 1]
                framed[b, at + length : at + length + 1] = across[after : after + 1]
                boxed.append(
                    framed[b, at - 1 : at - 1 + length]
                    + framed[b, at : at + length]
                    + framed[b, at + 1 : at + 1 + length]
                )
                at = at + length + 8
            boxed = jnp.concatenate(boxed, axis=0) if len(boxed) > 1 else boxed[0]
            scale = 1.0 / jnp.sqrt(boxed / (9.0 * channels) + width * width * epsilon)
            kept = result.at[2 * s + b] if last is None or s < 2 else last.at[b]
            for c in range(channels):
                kept[c] = result[2 * s + b, c] * scale
            finished(s, b)


def inner_kernel(
    edge_ref, middle_ref, far_middle_ref, ra_ref, dec_ref, box_ref, gather_ref,
    out_ref, last_ref, done_ref, edges_ref,
    source, smooth, result, framed, sems,
    *, batch,
):
    channels = 2 * edge_ref.shape[0]
    near = (lax.axis_index("ra") // 4) % 2
    edges_ref[...] = jnp.zeros_like(edges_ref)
    halves_of = ((edge_ref, HALF), (middle_ref, HALF)), ((edge_ref, 0), (far_middle_ref, 0))
    for part, parts in enumerate(halves_of):
        half_z = near if part == 0 else 1 - near
        for step in range(channels // 2 // batch):
            channels_at = []
            for j in range(batch):
                i = step * batch + j
                for half, (ref, at) in enumerate(parts):
                    packed = ref[i, at + 32 : at + HALF, :]
                    for k in range(2):
                        main = ref[i, at + 16 * k : at + 16 * k + 16, :]
                        put_rows(
                            source.at[part], j * ROWS + 32 * half + 16 * k, main,
                            (packed, packed), (64 * k, 64 * k + 32),
                        )
                channels_at.append((i, half_z))
            smooth_ra(source.at[part], ra_ref, ROWS, channels_at, done_ref, edges_ref)
    beside = functools.partial(beside_squares, [(dec_ref, edges_ref)], box_ref, gather_ref)

    copies = []

    def finished(s, b):
        if s == 2:
            return
        rows = pl.ds(EDGE, ROWS - 2 * EDGE)
        copy = pltpu.make_async_copy(
            result.at[2 * s + b], out_ref.at[s, b, :, rows, :], sems.at[2 * s + b]
        )
        copy.start()
        copies.append(copy)

    parts = [(dec_ref, done_ref)]
    snr_rows(parts, beside, (), inner_runs, smooth, result, framed, finished, last_ref)
    for copy in copies:
        copy.wait()


def outer_kernel(
    held_ref, last_ref, chip_ref, next_ref, done_ref, edges_ref,
    ra_ref, dec_ref, dec_halo_ref, box_ref, gather_ref,
    out_ref,
    source, halo_done, halo_edges, smooth, result, framed, sems,
    *, batch,
):
    copies = []

    def send(rows_ref, s, b, at):
        copy = pltpu.make_async_copy(
            rows_ref, out_ref.at[s, b, :, pl.ds(at, rows_ref.shape[1]), :], sems.at[len(copies)]
        )
        copy.start()
        copies.append(copy)

    del held_ref
    for b in range(2):
        send(last_ref.at[b], 2, b, EDGE)
    channels = done_ref.shape[2] // LANES
    near = (lax.axis_index("ra") // 4) % 2
    dec_at, dec_n = lax.axis_index("dec"), lax.axis_size("dec")
    halo_edges[...] = jnp.zeros_like(halo_edges)
    for step in range(channels // batch):
        channels_at = []
        for j in range(batch):
            at = step * batch + j
            part, i = at // (channels // 2), at % (channels // 2)
            for k, ref in enumerate((chip_ref, next_ref)):
                row = channels * EDGE + 8 * (at // 2)
                packed = ref[row : row + 8, :]
                lanes = 64 * (at % 2)
                put_rows(
                    source.at[step % 2], 2 * EDGE * j + EDGE * k, ref[at * EDGE : (at + 1) * EDGE, :],
                    (packed, packed), (lanes, lanes + 32),
                )
            half_z = near if part == 0 else 1 - near
            channels_at.append((i, half_z))
        smooth_ra(source.at[step % 2], ra_ref, 2 * EDGE, channels_at, halo_done, halo_edges)
    dec_halo_ref = dec_halo_ref.at[dec_at % 2]
    parts = [(dec_ref, done_ref), (dec_halo_ref, halo_done)]
    beside = functools.partial(
        beside_squares, [(dec_ref, edges_ref), (dec_halo_ref, halo_edges)], box_ref, gather_ref
    )

    def finished(s, b):
        for k, (first, length, _, _) in enumerate(outer_runs):
            rows_ref = result.at[2 * s + b, :, pl.ds(first, length), :]
            send(rows_ref, s, b, (0, ROWS - EDGE)[k])

    outside = ((32, dec_at == 0), (35, dec_at == dec_n - 1))
    snr_rows(parts, beside, outside, outer_runs, smooth, result, framed, finished)
    for copy in copies:
        copy.wait()


def local(cube):
    tiles = channels = lax.axis_size("ra")
    vmem = pl.BlockSpec(memory_space=pltpu.VMEM)
    f32 = jnp.float32

    def call(kernel, shapes, operands, name, outside=(), scratch=()):
        return pl.pallas_call(
            kernel,
            out_shape=shapes,
            in_specs=[pl.BlockSpec(memory_space=pl.ANY)] * len(outside) + [vmem] * len(operands),
            out_specs=jax.tree.map(lambda _: vmem, shapes),
            scratch_shapes=scratch,
            compiler_params=pltpu.CompilerParams(vmem_limit_bytes=32 * 2**20),
            name=name,
        )(*outside, *operands)

    across = [(i, i ^ 4) for i in range(tiles)]
    groups = [[8 * x + 4 * z + y for x in range(tiles // 8) for y in range(4)] for z in range(2)]

    def regroup(chunks):
        return lax.all_to_all(
            chunks, "ra", split_axis=0, concat_axis=0, tiled=True, axis_index_groups=groups
        )

    part = jax.ShapeDtypeStruct((tiles // 2 + 1, 32, LANES), f32)
    chunk = jax.ShapeDtypeStruct((tiles // 2, CHUNK, LANES), f32)
    rows = [pltpu.VMEM((32, cube.shape[2]), f32), pltpu.SemaphoreType.DMA((2,))]
    columns = functools.partial(column_kernel, tiles)
    part, near_part = call(columns, (part, part), (), "columns", (cube,), rows)
    part = lax.ppermute(part, "ra", across)

    def regroup_middle(cube):
        chunks = call(functools.partial(middle_kernel, tiles), chunk, (), "middle", (cube,), rows)
        return regroup(chunks)

    def nothing(cube):
        return jnp.zeros(chunk.shape, f32)

    middle = lax.cond(lax.axis_index("ra") >= 0, regroup_middle, nothing, cube)
    far_middle = lax.ppermute(middle[:, :HALF], "ra", across)

    def regroup_edges(part, near_part, middle):
        chunks = call(edge_rows_kernel, chunk, (part, near_part), "edge_rows", (middle,))
        return regroup(chunks)

    def no_edges(part, near_part, middle):
        return jnp.zeros(chunk.shape, f32)

    edge = jax.ShapeDtypeStruct((channels * (EDGE + 4), LANES), f32)
    edge_chunk = lax.cond(
        lax.axis_index("ra") >= 0, regroup_edges, no_edges, part, near_part, middle
    )
    for_chip, for_next, edge_chunk = call(
        edge_kernel, (edge, edge, chunk), (), "edges", (edge_chunk,), [pltpu.SemaphoreType.DMA]
    )
    count = lax.axis_size("dec")
    on_chip = [(i, i ^ 1) for i in range(count)]
    beyond = [(i, i + 1) for i in range(1, count - 1, 2)] + [(i + 1, i) for i in range(1, count - 1, 2)]
    from_chip = lax.ppermute(for_chip, "dec", on_chip)
    from_next = lax.ppermute(for_next, "dec", beyond)
    box, gather = (jnp.asarray(value) for value in edge_weights(channels))
    along = jnp.asarray(ra_weights())
    anywhere = pl.BlockSpec(memory_space=pl.ANY)
    out = jax.ShapeDtypeStruct((3, 2, channels, ROWS, LANES), f32)
    batch = 8
    smooth = pltpu.VMEM((2, OUT, channels * LANES), f32)
    framed = pltpu.VMEM((2, ROWS + 16, LANES), f32)
    result = (6, channels, 2 * EDGE, LANES)
    params = pltpu.CompilerParams(vmem_limit_bytes=32 * 2**20)
    held, last, done, edges = pl.pallas_call(
        functools.partial(inner_kernel, batch=batch),
        out_shape=(
            out,
            jax.ShapeDtypeStruct((2, *result[1:]), f32),
            jax.ShapeDtypeStruct((3, 2 * ROWS, channels * LANES), jnp.bfloat16),
            jax.ShapeDtypeStruct((2, ROWS, LANES), f32),
        ),
        in_specs=[vmem] * 7,
        out_specs=(anywhere, vmem, vmem, vmem),
        scratch_shapes=[
            pltpu.VMEM((2, batch * ROWS, 3 * LANES), jnp.bfloat16),
            smooth,
            pltpu.VMEM(result, f32),
            framed,
            pltpu.SemaphoreType.DMA((4,)),
        ],
        compiler_params=params,
        cost_estimate=pl.CostEstimate(
            flops=2 * 10**9, bytes_accessed=8 * 2**20, transcendentals=0
        ),
        name="inner",
    )(
        edge_chunk, middle, far_middle, along,
        jnp.asarray(dec_weights(inner_out, tile_rows)), box, gather,
    )
    batch = 16
    halo_weights = np.stack(
        [dec_weights(outer_out, rows) for rows in (below_rows + above_rows, above_rows + below_rows)]
    )
    return pl.pallas_call(
        functools.partial(outer_kernel, batch=batch),
        out_shape=out,
        in_specs=[anywhere] + [vmem] * 10,
        out_specs=anywhere,
        scratch_shapes=[
            pltpu.VMEM((2, batch * 2 * EDGE, 3 * LANES), jnp.bfloat16),
            pltpu.VMEM((3, 4 * EDGE, channels * LANES), jnp.bfloat16),
            pltpu.VMEM((2, 2 * EDGE, LANES), f32),
            smooth,
            pltpu.VMEM(result, f32),
            framed,
            pltpu.SemaphoreType.DMA((14,)),
        ],
        input_output_aliases={0: 0},
        compiler_params=params,
        cost_estimate=pl.CostEstimate(
            flops=10**9, bytes_accessed=8 * 2**20, transcendentals=0
        ),
        name="outer",
    )(
        held, last, from_chip, from_next, done, edges, along,
        jnp.asarray(dec_weights(outer_out, tile_rows)),
        jnp.asarray(halo_weights), box, gather,
    )


def solution(mesh):
    return jax.shard_map(
        local,
        mesh=mesh,
        in_specs=(P("ra", "dec", None),),
        out_specs=P(None, None, None, "dec", "ra"),
        check_vma=False,
    )
```

```python
import functools

import jax
import jax.numpy as jnp
import ml_dtypes
import numpy as np
from jax import lax
from jax.experimental import pallas as pl
from jax.experimental.pallas import tpu as pltpu
from jax.sharding import PartitionSpec as P

sigma_values = (1, 2, 4)
boxcar_widths = (3, 7)
epsilon = 1e-06

LANES = 128
ROWS = 64
EDGE = 16
OUT = 40
STEP = 1024
HALF = 40
CHUNK = 2 * HALF
edge_rows = tuple(range(0, EDGE)) + tuple(range(ROWS - EDGE, ROWS))
middle_rows = tuple(range(EDGE, ROWS - EDGE))
tile_rows = edge_rows + middle_rows
NEED = 3 * max(sigma_values) + 1
far_away = (1000,) * (EDGE - NEED)
above_rows = tuple(range(-NEED, 0)) + far_away
below_rows = tuple(range(ROWS, ROWS + NEED)) + far_away
inner_out = middle_rows + (EDGE - 1, ROWS - EDGE)
outer_out = edge_rows + (-1, EDGE, ROWS - EDGE - 1, ROWS)
inner_runs = ((0, 32, 32, 33),)
outer_runs = ((0, 16, 32, 33), (16, 16, 34, 35))
beside_cols = np.array(tuple(range(LANES, LANES + 16)) + tuple(range(-16, 0)))


def taps(distance, sigma):
    reach = 3 * sigma
    lags = np.arange(-reach, reach + 1, dtype=np.float64)
    weight_sum = np.sum(np.exp(-lags * lags / (2.0 * sigma * sigma)))
    value = np.exp(-(distance.astype(np.float64) ** 2) / (2.0 * sigma * sigma)) / weight_sum
    return np.where(np.abs(distance) <= reach, value, 0.0).astype(np.float32)


def halves(value):
    high = value.astype(ml_dtypes.bfloat16)
    low = (value - high.astype(np.float32)).astype(ml_dtypes.bfloat16)
    return high, low


def ra_weights():
    def band(cols):
        weights = np.zeros((len(cols), 4 * LANES), np.float32)
        for s, sigma in enumerate(sigma_values):
            weights[:, s * LANES : (s + 1) * LANES] = taps(
                cols[:, None] - np.arange(LANES)[None, :], sigma
            )
            for side, col in enumerate((-1, LANES)):
                weights[:, 3 * LANES + 32 * s + side] = taps(cols - col, sigma)
        return halves(weights)

    high, low = band(np.arange(LANES))
    beside_high, beside_low = band(beside_cols)
    nothing = np.zeros_like(beside_high)
    parts = [high, high, low, beside_high, beside_high, beside_low, nothing]
    return np.concatenate(parts, axis=0)


def dec_weights(out_rows, in_rows):
    result = np.zeros((3, 2 * OUT, 2 * len(in_rows)), ml_dtypes.bfloat16)
    for s, sigma in enumerate(sigma_values):
        weights = taps(np.array(in_rows)[None, :] - np.array(out_rows)[:, None], sigma)
        high, low = halves(weights)
        result[s, : len(out_rows), : len(in_rows)] = high
        result[s, : len(out_rows), len(in_rows) :] = high
        result[s, OUT : OUT + len(out_rows), : len(in_rows)] = low
    return result


def edge_weights(channels):
    half = channels // 2
    lane = np.arange(2 * LANES)
    tile, within = lane // LANES, lane % LANES
    sigma, slot = within // 32, within % 32
    channel, side = tile * half + slot // 2, slot % 2
    used = (sigma < 3) & (slot < 2 * half)
    same = used[:, None] & used[None, :] & (sigma[:, None] == sigma[None, :])
    same &= side[:, None] == side[None, :]
    boxcars = [
        same & (np.abs(channel[:, None] - channel[None, :]) <= width // 2)
        for width in boxcar_widths
    ]
    gathers = np.zeros((3, 2 * LANES, LANES), bool)
    for s in range(3):
        gathers[s, :, 0] = used & (sigma == s) & (side == 0)
        gathers[s, :, LANES - 1] = used & (sigma == s) & (side == 1)
    return (
        np.concatenate(boxcars, axis=1).astype(ml_dtypes.bfloat16),
        np.concatenate(gathers, axis=1).astype(ml_dtypes.bfloat16),
    )


def lane_index(shape):
    return lax.broadcasted_iota(jnp.int32, shape, len(shape) - 1)


def split(value):
    high = value.astype(jnp.bfloat16)
    low = (value - high.astype(jnp.float32)).astype(jnp.bfloat16)
    return high, low


def dot(a, b):
    return jnp.dot(a, b, preferred_element_type=jnp.float32)


def pack_rows(block, out_ref, tile, at):
    lane = lane_index((8, LANES))
    here, right, left = block
    packed = jnp.zeros((8, LANES), jnp.float32)
    for group in range(4):
        out_ref[tile, at + 8 * group : at + 8 * group + 8, :] = here(group)
        first, first_at = right(group)
        last, last_at = left(group)
        first = turn(first, 32 * group - first_at)
        last = turn(last, 32 * group + 16 - last_at)
        lanes = lane - 32 * group
        packed = jnp.where((lanes >= 0) & (lanes < 16), first, packed)
        packed = jnp.where((lanes >= 16) & (lanes < 32), last, packed)
    out_ref[tile, at + 32 : at + HALF, :] = packed


def turn(value, lanes):
    lanes = lanes % LANES
    return pltpu.roll(value, lanes, 1) if lanes else value


def far_half():
    return 1 - (lax.axis_index("ra") // 4) % 2


def rows_copies(cube_ref, rows, held, sems):
    copies = []
    for k, at in enumerate(range(0, len(rows), 16)):
        source = cube_ref.at[0, pl.ds(rows[at], 16), :]
        copies.append(pltpu.make_async_copy(source, held.at[pl.ds(at, 16), :], sems.at[k]))
    for copy in copies:
        copy.start()
    return copies


def column_kernel(tiles, cube_ref, far_ref, near_ref, held, sems):
    copies = rows_copies(cube_ref, edge_rows, held, sems)
    far = far_half()
    lane = lane_index((8, LANES))
    wide = tiles // 8

    def columns(tile, at):
        return held[at : at + 8, pl.ds(pl.multiple_of(tile * LANES, LANES), LANES)]

    for group in range(4):
        at = 8 * group
        if group % 2 == 0:
            copies[group // 2].wait()
        for half_z, out_ref in ((far, far_ref), (1 - far, near_ref)):
            beside = jnp.zeros((8, LANES), jnp.float32)
            for x in range(wide):
                first = 8 * x + 4 * half_z
                for y in range(4):
                    out_ref[4 * x + y, at : at + 8, :] = columns(first + y, at)
                right = turn(columns(jnp.minimum(first + 4, tiles - 1), at), 32 * x)
                left = turn(columns(jnp.maximum(first - 1, 0), at), 32 * x + 32)
                right = jnp.where(first + 4 < tiles, right, 0.0)
                left = jnp.where(first > 0, left, 0.0)
                lanes = lane - 32 * x
                beside = jnp.where((lanes >= 0) & (lanes < 16), right, beside)
                beside = jnp.where((lanes >= 16) & (lanes < 32), left, beside)
            out_ref[4 * wide, at : at + 8, :] = beside


def pack_cube(tiles, held, half_z, out_ref, at):
    def columns(tile, group):
        inside = (tile >= 0) & (tile < tiles)
        tile = jnp.clip(tile, 0, tiles - 1)
        lanes = pl.ds(pl.multiple_of(tile * LANES, LANES), LANES)
        return inside, held[8 * group : 8 * group + 8, lanes]

    for x in range(tiles // 8):
        for y in range(4):
            tile = 8 * x + 4 * half_z + y

            def here(group):
                return columns(tile, group)[1]

            def right(group):
                inside, value = columns(tile + 1, group)
                return (jnp.where(inside, value, 0.0) if y == 3 else value), 0

            def left(group):
                inside, value = columns(tile - 1, group)
                return (jnp.where(inside, value, 0.0) if y == 0 else value), LANES - 16

            pack_rows((here, right, left), out_ref, 4 * x + y, at)


def middle_kernel(tiles, cube_ref, out_ref, held, sems):
    for copy in rows_copies(cube_ref, middle_rows, held, sems):
        copy.wait()
    far = far_half()
    pack_cube(tiles, held, far, out_ref, 0)
    pack_cube(tiles, held, 1 - far, out_ref, HALF)


def edge_rows_kernel(after_ref, far_ref, near_ref, out_ref):
    del after_ref
    wide = out_ref.shape[0] // 4
    for start, ref in ((0, far_ref), (HALF, near_ref)):
        for x in range(wide):
            for y in range(4):
                tile = 4 * x + y

                def here(group):
                    return ref[tile, 8 * group : 8 * group + 8, :]

                def right(group):
                    if y < 3:
                        return ref[tile + 1, 8 * group : 8 * group + 8, :], 0
                    return ref[4 * wide, 8 * group : 8 * group + 8, :], 32 * x

                def left(group):
                    if y > 0:
                        return ref[tile - 1, 8 * group : 8 * group + 8, :], LANES - 16
                    return ref[4 * wide, 8 * group : 8 * group + 8, :], 32 * x + 16

                pack_rows((here, right, left), out_ref, tile, start)


def edge_kernel(outside_ref, chip_ref, next_ref, edge_ref, sem):
    fetch = pltpu.make_async_copy(outside_ref, edge_ref, sem)
    fetch.start()
    fetch.wait()
    odd = lax.axis_index("dec") % 2
    count = edge_ref.shape[0]
    channels = 2 * count
    lane = lane_index((8, LANES))
    row = lax.broadcasted_iota(jnp.int32, (8, LANES), 0)
    for ref, lower in ((chip_ref, 1 - odd), (next_ref, odd)):
        for part, start in enumerate((HALF, 0)):
            for i in range(count):
                at = (part * count + i) * NEED
                upper_rows = edge_ref[i, start : start + NEED, :]
                lower_rows = edge_ref[i, start + 2 * EDGE - NEED : start + 2 * EDGE, :]
                ref[at : at + NEED, :] = jnp.where(lower == 1, lower_rows, upper_rows)
            for pair in range(count // 2):
                at = channels * NEED + 8 * (part * count // 2 + pair)
                first = edge_ref[2 * pair, start + 32 : start + HALF, :]
                second = edge_ref[2 * pair + 1, start + 32 : start + HALF, :]
                upper_halves = jnp.where(lane < 64, first, pltpu.roll(second, 64, 1))
                lower_halves = jnp.where(lane < 64, pltpu.roll(first, 64, 1), second)
                lower_halves = pltpu.roll(lower_halves, 8 - (EDGE - NEED), 0)
                follows = (row >= 8 - (EDGE - NEED)) & (lane // 32 % 2 == 0)
                lower_halves = jnp.where(
                    follows, pltpu.roll(lower_halves, LANES - 32, 1), lower_halves
                )
                ref[at : at + 8, :] = jnp.where(lower == 1, lower_halves, upper_halves)


def put_rows(source, at, main, packed, places):
    lane = lane_index((8, LANES))
    high, low = split(main)
    beside = []
    for value, place in zip(packed, places):
        value_high = value.astype(jnp.bfloat16).astype(jnp.float32)
        value_low = value - value_high
        mix = jnp.where(lane < 64, turn(value_low, 32 - place), turn(value_high, 64 - place))
        mix = jnp.where(lane < 32, turn(value_high, -place), mix)
        beside.append(jnp.where(lane < 96, mix, 0.0))
    source[at : at + 16, :LANES] = low
    source[at : at + 16, LANES : 2 * LANES] = high
    source[at : at + 16, 2 * LANES :] = jnp.concatenate(beside, axis=0).astype(jnp.bfloat16)


def smooth_ra(source, weights_ref, rows, channels_at, done, edges):
    operand = jnp.concatenate([source[:, : 2 * LANES], source[:, LANES:]], axis=1)
    along = dot(operand, weights_ref[...])
    beside = {}
    for j, (i, half_z) in enumerate(channels_at):
        c = 8 * (i // 4) + 4 * half_z + i % 4
        block = along[j * rows : (j + 1) * rows]
        lanes = pl.ds(pl.multiple_of(c * LANES, LANES), LANES)
        for s in range(3):
            high, low = split(block[:, s * LANES : (s + 1) * LANES])
            done[s, :rows, lanes] = high
            done[s, rows:, lanes] = low
        value = turn(block[:, 3 * LANES :], 16 * (i // 4 % 2) + 2 * (i % 4))
        beside[i // 8] = beside[i // 8] + value if i // 8 in beside else value
    for tile, value in beside.items():
        edges[tile] = edges[tile] + pltpu.roll(value, 8 * half_z, 1)


def smooth_dec(parts, s, out):
    for at in range(0, out.shape[1], STEP):
        both = sum(dot(weights[s], done[s, :, at : at + STEP]) for weights, done in parts)
        out[:, at : at + STEP] = both[:OUT] + both[OUT:]


def beside_squares(parts, box_ref, gather_ref):
    which = lane_index((OUT, 2 * LANES)) % LANES // 32
    smoothed = jnp.zeros((OUT, 2 * LANES), jnp.float32)
    parts = [
        (weights, jnp.concatenate(split(jnp.concatenate([edges[0], edges[1]], axis=1)), axis=0))
        for weights, edges in parts
    ]
    for s in range(3):
        both = sum(dot(weights[s], value) for weights, value in parts)
        smoothed = jnp.where(which == s, both[:OUT] + both[OUT:], smoothed)
    high, low = split(smoothed)
    summed = dot(high, box_ref[...]) + dot(low, box_ref[...])
    summed = jnp.concatenate([summed[:, : 2 * LANES], summed[:, 2 * LANES :]], axis=0)
    high, low = split(summed * summed)
    squares = dot(high, gather_ref[...]) + dot(low, gather_ref[...])
    return [
        [squares[b * OUT : (b + 1) * OUT, s * LANES : (s + 1) * LANES] for s in range(3)]
        for b in range(2)
    ]


def boxcar_sums(smooth, rows, result):
    channels = result.shape[1]
    squares = [[], []]
    for at in range(0, OUT, 8):
        planes = {
            c: smooth[at : at + 8, c * LANES : (c + 1) * LANES] for c in range(channels)
        }

        def total(places):
            return functools.reduce(jnp.add, [planes[c] for c in places if c in planes])

        triples = {c: total(range(c - 1, c + 2)) for c in range(-1, channels + 1)}
        totals = [[None, None], [None, None]]
        for c in range(channels):
            terms = [triples[c - 2]] if c >= 1 else []
            terms += [triples[c + 1]] + ([planes[c + 3]] if c + 3 < channels else [])
            for b, value in enumerate((triples[c], functools.reduce(jnp.add, terms))):
                if at < rows:
                    result[b, c, at : at + 8, :] = value
                square = value * value
                before = totals[b][c % 2]
                totals[b][c % 2] = square if before is None else before + square
        for b in range(2):
            squares[b].append(totals[b][0] + totals[b][1])
    return [jnp.concatenate(square, axis=0) for square in squares]


def snr_rows(parts, beside, outside, runs, smooth, result, framed, finished, last=None):
    channels = result.shape[1]
    ra_at, ra_n = lax.axis_index("ra"), lax.axis_size("ra")
    lane = lane_index((OUT, LANES))
    row = lax.broadcasted_iota(jnp.int32, (OUT, LANES), 0)
    gone = row < 0
    for at, condition in outside:
        gone = gone | ((row == at) & condition)
    no_side = ((lane == 0) & (ra_at == 0)) | ((lane == LANES - 1) & (ra_at == ra_n - 1))
    rows = sum(run[1] for run in runs)
    smooth_dec(parts, 0, smooth.at[0])
    for s in range(3):
        if s == 1:
            smooth_dec(parts, 2, smooth.at[0])
        squares = boxcar_sums(smooth.at[s % 2], rows, result.at[pl.ds(2 * s, 2)])
        if s == 0:
            beside = beside()
            smooth_dec(parts, 1, smooth.at[1])
        for b, width in enumerate(boxcar_widths):
            square = jnp.where(gone, 0.0, squares[b])
            across = square + jnp.where(no_side | gone, 0.0, beside[b][s])
            across = across + jnp.where(lane == 0, 0.0, pltpu.roll(square, 1, 1))
            across = across + jnp.where(lane == LANES - 1, 0.0, pltpu.roll(square, LANES - 1, 1))
            boxed = []
            at = 0
            for first, length, before, after in runs:
                at = at + 8
                framed[b, at : at + length] = across[first : first + length]
                framed[b, at - 1 : at] = across[before : before + 1]
                framed[b, at + length : at + length + 1] = across[after : after + 1]
                boxed.append(
                    framed[b, at - 1 : at - 1 + length]
                    + framed[b, at : at + length]
                    + framed[b, at + 1 : at + 1 + length]
                )
                at = at + length + 8
            boxed = jnp.concatenate(boxed, axis=0) if len(boxed) > 1 else boxed[0]
            scale = 1.0 / jnp.sqrt(boxed / (9.0 * channels) + width * width * epsilon)
            kept = result.at[2 * s + b] if last is None or s < 2 else last.at[b]
            for c in range(channels):
                kept[c] = result[2 * s + b, c] * scale
            finished(s, b)


def inner_kernel(
    edge_ref, middle_ref, far_middle_ref, ra_ref, dec_ref, box_ref, gather_ref,
    out_ref, last_ref, done_ref, edges_ref,
    source, smooth, result, framed, sems,
    *, batch,
):
    channels = 2 * edge_ref.shape[0]
    near = (lax.axis_index("ra") // 4) % 2
    edges_ref[...] = jnp.zeros_like(edges_ref)
    halves_of = ((edge_ref, HALF), (middle_ref, HALF)), ((edge_ref, 0), (far_middle_ref, 0))
    for part, parts in enumerate(halves_of):
        half_z = near if part == 0 else 1 - near
        for step in range(channels // 2 // batch):
            channels_at = []
            for j in range(batch):
                i = step * batch + j
                for half, (ref, at) in enumerate(parts):
                    packed = ref[i, at + 32 : at + HALF, :]
                    for k in range(2):
                        main = ref[i, at + 16 * k : at + 16 * k + 16, :]
                        put_rows(
                            source.at[part], j * ROWS + 32 * half + 16 * k, main,
                            (packed, packed), (64 * k, 64 * k + 32),
                        )
                channels_at.append((i, half_z))
            smooth_ra(source.at[part], ra_ref, ROWS, channels_at, done_ref, edges_ref)
    beside = functools.partial(beside_squares, [(dec_ref, edges_ref)], box_ref, gather_ref)

    copies = []

    def finished(s, b):
        if s == 2:
            return
        rows = pl.ds(EDGE, ROWS - 2 * EDGE)
        copy = pltpu.make_async_copy(
            result.at[2 * s + b], out_ref.at[s, b, :, rows, :], sems.at[2 * s + b]
        )
        copy.start()
        copies.append(copy)

    parts = [(dec_ref, done_ref)]
    snr_rows(parts, beside, (), inner_runs, smooth, result, framed, finished, last_ref)
    for copy in copies:
        copy.wait()


def outer_kernel(
    held_ref, last_ref, chip_ref, next_ref, done_ref, edges_ref,
    ra_ref, dec_ref, dec_halo_ref, box_ref, gather_ref,
    out_ref,
    source, halo_done, halo_edges, smooth, result, framed, sems,
    *, batch,
):
    copies = []

    def send(rows_ref, s, b, at):
        copy = pltpu.make_async_copy(
            rows_ref, out_ref.at[s, b, :, pl.ds(at, rows_ref.shape[1]), :], sems.at[len(copies)]
        )
        copy.start()
        copies.append(copy)

    del held_ref
    for b in range(2):
        send(last_ref.at[b], 2, b, EDGE)
    channels = done_ref.shape[2] // LANES
    near = (lax.axis_index("ra") // 4) % 2
    dec_at, dec_n = lax.axis_index("dec"), lax.axis_size("dec")
    halo_edges[...] = jnp.zeros_like(halo_edges)
    for step in range(channels // batch):
        channels_at = []
        for j in range(batch):
            at = step * batch + j
            part, i = at // (channels // 2), at % (channels // 2)
            for k, ref in enumerate((chip_ref, next_ref)):
                row = channels * NEED + 8 * (at // 2)
                packed = ref[row : row + 8, :]
                lanes = 64 * (at % 2)
                put_rows(
                    source.at[step % 2], 2 * EDGE * j + EDGE * k, ref[at * NEED : at * NEED + EDGE, :],
                    (packed, packed), (lanes, lanes + 32),
                )
            half_z = near if part == 0 else 1 - near
            channels_at.append((i, half_z))
        smooth_ra(source.at[step % 2], ra_ref, 2 * EDGE, channels_at, halo_done, halo_edges)
    dec_halo_ref = dec_halo_ref.at[dec_at % 2]
    parts = [(dec_ref, done_ref), (dec_halo_ref, halo_done)]
    beside = functools.partial(
        beside_squares, [(dec_ref, edges_ref), (dec_halo_ref, halo_edges)], box_ref, gather_ref
    )

    def finished(s, b):
        for k, (first, length, _, _) in enumerate(outer_runs):
            rows_ref = result.at[2 * s + b, :, pl.ds(first, length), :]
            send(rows_ref, s, b, (0, ROWS - EDGE)[k])

    outside = ((32, dec_at == 0), (35, dec_at == dec_n - 1))
    snr_rows(parts, beside, outside, outer_runs, smooth, result, framed, finished)
    for copy in copies:
        copy.wait()


def local(cube):
    tiles = channels = lax.axis_size("ra")
    vmem = pl.BlockSpec(memory_space=pltpu.VMEM)
    f32 = jnp.float32

    def call(kernel, shapes, operands, name, outside=(), scratch=()):
        return pl.pallas_call(
            kernel,
            out_shape=shapes,
            in_specs=[pl.BlockSpec(memory_space=pl.ANY)] * len(outside) + [vmem] * len(operands),
            out_specs=jax.tree.map(lambda _: vmem, shapes),
            scratch_shapes=scratch,
            compiler_params=pltpu.CompilerParams(vmem_limit_bytes=32 * 2**20),
            name=name,
        )(*outside, *operands)

    across = [(i, i ^ 4) for i in range(tiles)]
    groups = [[8 * x + 4 * z + y for x in range(tiles // 8) for y in range(4)] for z in range(2)]

    def regroup(chunks):
        return lax.all_to_all(
            chunks, "ra", split_axis=0, concat_axis=0, tiled=True, axis_index_groups=groups
        )

    part = jax.ShapeDtypeStruct((tiles // 2 + 1, 32, LANES), f32)
    chunk = jax.ShapeDtypeStruct((tiles // 2, CHUNK, LANES), f32)
    rows = [pltpu.VMEM((32, cube.shape[2]), f32), pltpu.SemaphoreType.DMA((2,))]
    columns = functools.partial(column_kernel, tiles)
    part, near_part = call(columns, (part, part), (), "columns", (cube,), rows)
    part = lax.ppermute(part, "ra", across)

    def regroup_middle(cube):
        chunks = call(functools.partial(middle_kernel, tiles), chunk, (), "middle", (cube,), rows)
        return regroup(chunks)

    def nothing(cube):
        return jnp.zeros(chunk.shape, f32)

    middle = lax.cond(lax.axis_index("ra") >= 0, regroup_middle, nothing, cube)
    far_middle = lax.ppermute(middle[:, :HALF], "ra", across)

    def regroup_edges(part, near_part, middle):
        chunks = call(edge_rows_kernel, chunk, (part, near_part), "edge_rows", (middle,))
        return regroup(chunks)

    def no_edges(part, near_part, middle):
        return jnp.zeros(chunk.shape, f32)

    edge = jax.ShapeDtypeStruct((channels * (NEED + 4), LANES), f32)
    edge_chunk = lax.cond(
        lax.axis_index("ra") >= 0, regroup_edges, no_edges, part, near_part, middle
    )
    for_chip, for_next, edge_chunk = call(
        edge_kernel, (edge, edge, chunk), (), "edges", (edge_chunk,), [pltpu.SemaphoreType.DMA]
    )
    count = lax.axis_size("dec")
    on_chip = [(i, i ^ 1) for i in range(count)]
    beyond = [(i, i + 1) for i in range(1, count - 1, 2)] + [(i + 1, i) for i in range(1, count - 1, 2)]
    from_chip = lax.ppermute(for_chip, "dec", on_chip)
    from_next = lax.ppermute(for_next, "dec", beyond)
    box, gather = (jnp.asarray(value) for value in edge_weights(channels))
    along = jnp.asarray(ra_weights())
    anywhere = pl.BlockSpec(memory_space=pl.ANY)
    out = jax.ShapeDtypeStruct((3, 2, channels, ROWS, LANES), f32)
    batch = 8
    smooth = pltpu.VMEM((2, OUT, channels * LANES), f32)
    framed = pltpu.VMEM((2, ROWS + 16, LANES), f32)
    result = (6, channels, 2 * EDGE, LANES)
    params = pltpu.CompilerParams(vmem_limit_bytes=32 * 2**20)
    held, last, done, edges = pl.pallas_call(
        functools.partial(inner_kernel, batch=batch),
        out_shape=(
            out,
            jax.ShapeDtypeStruct((2, *result[1:]), f32),
            jax.ShapeDtypeStruct((3, 2 * ROWS, channels * LANES), jnp.bfloat16),
            jax.ShapeDtypeStruct((2, ROWS, LANES), f32),
        ),
        in_specs=[vmem] * 7,
        out_specs=(anywhere, vmem, vmem, vmem),
        scratch_shapes=[
            pltpu.VMEM((2, batch * ROWS, 3 * LANES), jnp.bfloat16),
            smooth,
            pltpu.VMEM(result, f32),
            framed,
            pltpu.SemaphoreType.DMA((4,)),
        ],
        compiler_params=params,
        cost_estimate=pl.CostEstimate(
            flops=2 * 10**9, bytes_accessed=8 * 2**20, transcendentals=0
        ),
        name="inner",
    )(
        edge_chunk, middle, far_middle, along,
        jnp.asarray(dec_weights(inner_out, tile_rows)), box, gather,
    )
    batch = 16
    halo_weights = np.stack(
        [dec_weights(outer_out, rows) for rows in (below_rows + above_rows, above_rows + below_rows)]
    )
    return pl.pallas_call(
        functools.partial(outer_kernel, batch=batch),
        out_shape=out,
        in_specs=[anywhere] + [vmem] * 10,
        out_specs=anywhere,
        scratch_shapes=[
            pltpu.VMEM((2, batch * 2 * EDGE, 3 * LANES), jnp.bfloat16),
            pltpu.VMEM((3, 4 * EDGE, channels * LANES), jnp.bfloat16),
            pltpu.VMEM((2, 2 * EDGE, LANES), f32),
            smooth,
            pltpu.VMEM(result, f32),
            framed,
            pltpu.SemaphoreType.DMA((14,)),
        ],
        input_output_aliases={0: 0},
        compiler_params=params,
        cost_estimate=pl.CostEstimate(
            flops=10**9, bytes_accessed=8 * 2**20, transcendentals=0
        ),
        name="outer",
    )(
        held, last, from_chip, from_next, done, edges, along,
        jnp.asarray(dec_weights(outer_out, tile_rows)),
        jnp.asarray(halo_weights), box, gather,
    )


def solution(mesh):
    return jax.shard_map(
        local,
        mesh=mesh,
        in_specs=(P("ra", "dec", None),),
        out_specs=P(None, None, None, "dec", "ra"),
        check_vma=False,
    )
```
